128 devices in a mesh: lat: 4 (over z), lon: 32 (over x, y, core).
Axes of the slice: x: 4, y: 4, z: 4, core: 2. Of those that a mesh axis runs over, the one named last changes fastest.
Arguments:
- fields: bfloat16 [4, 69, 96, 4096], P(None, None, 'lat', 'lon'), may hold values from -6 to 6
- conv_weight: bfloat16 [9, 128, 69], replicated, may hold values from -0.25 to 0.25
- kv_weight: bfloat16 [512, 128], replicated, may hold values from -0.5 to 0.5
- out_weight: bfloat16 [256, 256], replicated, may hold values from -0.375 to 0.375
- norm_gain: float32 [256], replicated, may hold values from 0.5 to 1.5
- queries: bfloat16 [256, 256], replicated, may hold values from -64 to 64
Outputs:
- features: bfloat16 [4, 128, 96, 4096], P(None, None, 'lat', 'lon')
- latents: float32 [4, 256, 256], replicated
The draws below stay inside these ranges and needn't reach their ends.
All inputs are finite; a program needn't handle non-finite values.
Results may differ from the reference program's by a relative error of at most 0.0035.
The reference program's roundings to bfloat16 on the way count: a program that leaves them out, or rounds other values in their place, can miss the bound.
Values may be sent and summed in bfloat16 or wider, within the bound.
A program may use at most 320 MiB of HBM per device.

```python
import jax
import jax.numpy as jnp
from jax import lax

B = 4
C = 69
F = 128
DL = 256
Q = 256
HEADS = 4
HD = 64
BLK = 8
CLON = 128
NLAT = 96
NLON = 4096


def draw_queries(key, part):
    key_base = jax.random.fold_in(key, 11)
    standard = jax.random.normal(key_base, (Q, DL), jnp.float32) * 8.0
    values = jnp.clip(standard, -48.0, 48.0)
    return values.astype(jnp.bfloat16)


def block_scale(rng, shape, cuts, low, top_value):
    level, own = 1.0, jax.random.fold_in(rng, 6)
    for axis_at, parts in cuts:
        steps = jnp.exp(jax.random.uniform(jax.random.fold_in(own, axis_at), (parts,), jnp.float32, low / len(cuts), top_value / len(cuts)))
        level = level * jnp.repeat(steps, shape[axis_at] // parts).reshape([-1 if axis == axis_at else 1 for axis in range(len(shape))])
    return level


def gaussian(key, extent, width, limit, pieces=(), held_as=jnp.bfloat16):
    drawn = width * jax.random.normal(key, extent, jnp.float32)
    if pieces:
        drawn = drawn * block_scale(key, extent, pieces, -0.22, 0.18)
    return jnp.clip(drawn, -limit, limit).astype(held_as)


def setup_inputs(seed: int = 0) -> dict:
    arg_keys = jax.random.split(jax.random.key(seed), 7)
    fields = gaussian(arg_keys[0], (B, C, NLAT, NLON), 1.0, 6.0, ((2, 4), (3, 32)))
    conv_weight = gaussian(arg_keys[1], (9, F, C), (9 * C) ** -0.5, 0.25)
    kv_weight = gaussian(arg_keys[2], (2 * DL, F), F ** -0.5, 0.5)
    out_weight = gaussian(arg_keys[3], (DL, DL), DL ** -0.5, 0.375)
    norm_gain = jnp.clip(1.0 + 0.1 * jax.random.normal(arg_keys[4], (DL,), jnp.float32), 0.5, 1.5)
    queries = draw_queries(jax.random.fold_in(arg_keys[6], 71), 0)
    return dict(fields=fields, conv_weight=conv_weight, kv_weight=kv_weight, out_weight=out_weight, norm_gain=norm_gain, queries=queries)


def convolve_block(window_in, conv_weight, lat_rows, lon_cols):
    running = jnp.zeros((window_in.shape[0], conv_weight.shape[1], lat_rows, lon_cols), jnp.float32)
    for tap_index in range(9):
        row_off = tap_index // 3
        col_off = tap_index % 3
        piece = window_in[:, :, row_off:row_off + lat_rows, col_off:col_off + lon_cols]
        running = running + jnp.einsum('fc,bcin->bfin', conv_weight[tap_index].astype(jnp.float32), piece.astype(jnp.float32))
    return running

def block_terms(window_in, conv_weight, kv_weight, queries, lat_rows, lon_cols):
    samples = window_in.shape[0]
    convolved = convolve_block(window_in, conv_weight, lat_rows, lon_cols)
    block_features = jax.nn.gelu(convolved, approximate=True).astype(jnp.bfloat16)
    flattened = block_features.reshape(samples, block_features.shape[1], lat_rows * lon_cols)
    key_value = jnp.einsum('of,bfn->bon', kv_weight.astype(jnp.float32), flattened.astype(jnp.float32)).astype(jnp.bfloat16)
    key_heads = key_value[:, :DL].reshape(samples, HEADS, HD, lat_rows * lon_cols)
    value_heads = key_value[:, DL:].reshape(samples, HEADS, HD, lat_rows * lon_cols)
    query_heads = queries.reshape(Q, HEADS, HD)
    scores = jnp.einsum('qhd,bhdn->bhqn', query_heads.astype(jnp.float32), key_heads.astype(jnp.float32)) * HD ** (-0.5)
    maxima = lax.optimization_barrier(jnp.max(scores, axis=-1))
    exponent = jnp.exp(scores - maxima[..., None])
    totals = lax.optimization_barrier(jnp.sum(exponent, axis=-1))
    weights_bf = exponent.astype(jnp.bfloat16)
    weighted = jnp.einsum('bhqn,bhdn->bqhd', weights_bf.astype(jnp.float32), value_heads.astype(jnp.float32))
    return (block_features, maxima, totals, weighted.reshape(samples, Q, DL))

def reference(fields, conv_weight, kv_weight, out_weight, norm_gain, queries):
    wrapped = jnp.concatenate([fields[..., -1:], fields, fields[..., :1]], axis=3)
    padded = jnp.pad(wrapped, ((0, 0), (0, 0), (1, 1), (0, 0)))
    lat_blocks = NLAT // BLK
    lon_blocks = NLON // CLON

    def one_block(block_index):
        lat_block = block_index // lon_blocks
        lon_block = block_index % lon_blocks
        zero_index = jnp.zeros((), jnp.int32)
        window_in = lax.dynamic_slice(padded, (zero_index, zero_index, (lat_block * BLK).astype(jnp.int32), (lon_block * CLON).astype(jnp.int32)), (B, C, BLK + 2, CLON + 2))
        return block_terms(window_in, conv_weight, kv_weight, queries, BLK, CLON)
    feats, maxima, totals, weighted = lax.map(one_block, jnp.arange(lat_blocks * lon_blocks, dtype=jnp.int32))
    peak = lax.optimization_barrier(jnp.max(maxima, axis=0))
    factor = jnp.exp(maxima - peak[None])
    total_all = lax.optimization_barrier(jnp.sum(totals * factor, axis=0))
    count_all = weighted.shape[0]
    head_factor = jnp.transpose(factor, (0, 1, 3, 2))[..., None]
    weighted_all = lax.optimization_barrier(jnp.sum(weighted.reshape(count_all, B, Q, HEADS, HD) * head_factor, axis=0))
    attended = (weighted_all / jnp.transpose(total_all, (0, 2, 1))[..., None]).reshape(B, Q, DL).astype(jnp.bfloat16)
    projected = jnp.einsum('bqe,ef->bqf', attended.astype(jnp.float32), out_weight.astype(jnp.float32))
    latents = projected * lax.rsqrt(lax.optimization_barrier(jnp.mean(projected * projected, axis=-1, keepdims=True)) + 1e-06) * norm_gain.astype(jnp.float32)
    features = feats.reshape(lat_blocks, lon_blocks, B, F, BLK, CLON)
    features = jnp.transpose(features, (2, 3, 0, 4, 1, 5)).reshape(B, F, NLAT, NLON)
    return (features, latents)
```

```python
import functools
import jax
import jax.numpy as jnp
from jax import lax
from jax.experimental import pallas as pl
from jax.experimental.pallas import tpu as pltpu
from jax.sharding import PartitionSpec as P

DL = 256
Q = 256
HEADS = 4
HD = 64
BLK = 8
MESH = pl.DeviceIdType.MESH
ROWS = 8
NCHIP = 64


def reduce_kernel(
    w_ref, st_ref, ow_ref, gain_ref, out_ref,
    half_w, half_st, msg, recv, own, gath,
    sem_a, sem_b, sem_c,
):
    lat = lax.axis_index("lat")
    lon = lax.axis_index("lon")
    core = lax.rem(lon, 2)
    chip = lat * 16 + lon // 2
    partner = lon + 1 - 2 * core

    def peer(k):
        c = lax.rem(chip + k, NCHIP)
        return (c // 16, lax.rem(c, 16) * 2 + core)

    barrier = pltpu.get_barrier_semaphore()
    pl.semaphore_signal(barrier, inc=1, device_id=(lat, partner), device_id_type=MESH)

    def greet(k, _):
        pl.semaphore_signal(barrier, inc=1, device_id=peer(k), device_id_type=MESH)
        return 0

    lax.fori_loop(1, NCHIP, greet, 0)
    pl.semaphore_wait(barrier, NCHIP)

    give = 1 - core
    cw = pltpu.make_async_remote_copy(
        w_ref.at[give], half_w, sem_a.at[0], sem_a.at[1], device_id=(lat, partner), device_id_type=MESH)
    cs = pltpu.make_async_remote_copy(
        st_ref.at[give], half_st, sem_a.at[2], sem_a.at[3], device_id=(lat, partner), device_id_type=MESH)
    cs.start()
    cw.start()
    cs.wait()
    cw.wait()

    s1 = st_ref[core]
    s2 = half_st[...]
    peak = jnp.maximum(s1, s2)
    f1 = jnp.exp(s1 - peak)
    f2 = jnp.exp(s2 - peak)
    lane = lax.broadcasted_iota(jnp.int32, (512, 128), 1)
    t1 = pltpu.roll(s1, 124, 1)
    t2 = pltpu.roll(s2, 124, 1)
    tot = t1 * f1 + t2 * f2
    for h in range(4):
        cols = slice(h * 64, h * 64 + 64)
        val = w_ref[core, :, cols] * f1[:, h:h + 1] + half_w[:, cols] * f2[:, h:h + 1]
        msg[:, :, cols] = val.reshape(NCHIP, ROWS, 64).astype(jnp.bfloat16)

    def limbs(v):
        a = v.astype(jnp.bfloat16).astype(jnp.float32)
        b = (v - a).astype(jnp.bfloat16).astype(jnp.float32)
        return a, b, v - a - b

    m0, m1, m2 = limbs(jnp.where(lane < 4, peak, 0.0))
    q0, q1, q2 = limbs(jnp.where(lane < 4, tot, 0.0))
    packed = (m0 + pltpu.roll(m1, 4, 1) + pltpu.roll(m2, 8, 1)
              + pltpu.roll(q0, 12, 1) + pltpu.roll(q1, 16, 1) + pltpu.roll(q2, 20, 1))
    msg[:, :, 256:384] = packed.reshape(NCHIP, ROWS, 128).astype(jnp.bfloat16)

    def scatter(k, _):
        c = lax.rem(chip + k, NCHIP)
        pltpu.make_async_remote_copy(
            msg.at[c], recv.at[k - 1], sem_b.at[0], sem_b.at[1], device_id=peer(k), device_id_type=MESH).start()
        return 0

    lax.fori_loop(1, NCHIP, scatter, 0)
    own[...] = msg[chip]
    pltpu.make_async_copy(recv, recv, sem_b.at[1]).wait()

    def stats(v):
        m = v + pltpu.roll(v, 124, 1) + pltpu.roll(v, 120, 1)
        t = pltpu.roll(v, 116, 1) + pltpu.roll(v, 112, 1) + pltpu.roll(v, 108, 1)
        return m, t

    def unpack(buf):
        return buf.astype(jnp.float32)

    all_st = jnp.concatenate([recv[:, :, 256:384].astype(jnp.float32), own[:, 256:384].astype(jnp.float32)[None]], axis=0)
    am, at = stats(all_st.reshape(512, 128))
    am = am.reshape(NCHIP, ROWS, 128)
    at = at.reshape(NCHIP, ROWS, 128)
    top = jnp.max(am, axis=0)
    fac = jnp.exp(am - top[None])
    total = jnp.sum(fac * at, axis=0)
    for h in range(4):
        cols = slice(h * 64, h * 64 + 64)
        acc = (jnp.sum(recv[:, :, cols].astype(jnp.float32) * fac[:63, :, h:h + 1], axis=0)
               + own[:, cols].astype(jnp.float32) * fac[63, :, h:h + 1])
        gath[core * NCHIP + chip, :, cols] = (acc / total[:, h:h + 1]).astype(jnp.bfloat16)
    pltpu.make_async_copy(recv, recv, sem_b.at[0]).wait()

    mine = core * NCHIP + chip

    def spread(k, _):
        pltpu.make_async_remote_copy(
            gath.at[mine], gath.at[mine], sem_c.at[0], sem_c.at[1], device_id=peer(k), device_id_type=MESH).start()
        return 0

    lax.fori_loop(1, NCHIP, spread, 0)
    size = gath.at[pl.ds(0, NCHIP - 1)]
    pltpu.make_async_copy(size, size, sem_c.at[1]).wait()
    pltpu.make_async_copy(size, size, sem_c.at[0]).wait()
    block = gath.at[pl.ds(core * NCHIP, NCHIP)]
    cg = pltpu.make_async_remote_copy(
        block, block, sem_c.at[2], sem_c.at[3], device_id=(lat, partner), device_id_type=MESH)
    cg.start()
    cg.wait()
    att = gath[...].astype(jnp.float32).reshape(1024, 256).astype(jnp.bfloat16)
    proj = jnp.dot(att, ow_ref[...], preferred_element_type=jnp.float32)
    out_ref[...] = (
        proj * lax.rsqrt(jnp.mean(proj * proj, axis=-1, keepdims=True) + 1e-06) * gain_ref[...]
    )


def reduce_all(weighted, stats, out_weight, norm_gain):
    vm = pl.BlockSpec(memory_space=pltpu.VMEM)
    return pl.pallas_call(
        reduce_kernel,
        out_shape=jax.ShapeDtypeStruct((1024, 256), jnp.float32),
        in_specs=[vm] * 4,
        out_specs=vm,
        scratch_shapes=[
            pltpu.VMEM((512, 256), jnp.float32),
            pltpu.VMEM((512, 128), jnp.float32),
            pltpu.VMEM((NCHIP, ROWS, 384), jnp.bfloat16),
            pltpu.VMEM((NCHIP - 1, ROWS, 384), jnp.bfloat16),
            pltpu.VMEM((ROWS, 384), jnp.bfloat16),
            pltpu.VMEM((2 * NCHIP, ROWS, 256), jnp.bfloat16),
            pltpu.SemaphoreType.DMA((4,)),
            pltpu.SemaphoreType.DMA((2,)),
            pltpu.SemaphoreType.DMA((4,)),
        ],
        compiler_params=pltpu.CompilerParams(
            collective_id=1, has_side_effects=True, vmem_limit_bytes=32 * 1024 * 1024
        ),
    )(weighted.reshape(2, 512, 256), stats.reshape(2, 512, 128), out_weight, norm_gain.reshape(1, 256))


def extended(block, sides, width, periodic):
    for axis, dim in sides:
        count = lax.axis_size(axis)
        forward = [(i, i + 1) for i in range(count - 1)]
        if periodic:
            forward.append((count - 1, 0))
        backward = [(target, source) for source, target in forward]
        low = lax.ppermute(
            lax.slice_in_dim(block, block.shape[dim] - width, None, axis=dim), axis, forward
        )
        high = lax.ppermute(lax.slice_in_dim(block, 0, width, axis=dim), axis, backward)
        block = jnp.concatenate([low, block, high], axis=dim)
    return block


def convolve_block(window_in, conv_weight, lat_rows, lon_cols):
    running = jnp.zeros((window_in.shape[0], conv_weight.shape[1], lat_rows, lon_cols), jnp.float32)
    for tap_index in range(9):
        row_off = tap_index // 3
        col_off = tap_index % 3
        piece = window_in[:, :, row_off : row_off + lat_rows, col_off : col_off + lon_cols]
        running = running + jnp.einsum(
            "fc,bcin->bfin", conv_weight[tap_index], piece, preferred_element_type=jnp.float32
        )
    return running


def block_terms(window_in, conv_weight, kv_weight, queries, lat_rows, lon_cols):
    samples = window_in.shape[0]
    convolved = convolve_block(window_in, conv_weight, lat_rows, lon_cols)
    block_features = jax.nn.gelu(convolved, approximate=True).astype(jnp.bfloat16)
    flattened = block_features.reshape(samples, block_features.shape[1], lat_rows * lon_cols)
    key_value = jnp.einsum(
        "of,bfn->bon", kv_weight, flattened, preferred_element_type=jnp.float32
    ).astype(jnp.bfloat16)
    key_heads = key_value[:, :DL].reshape(samples, HEADS, HD, lat_rows * lon_cols)
    value_heads = key_value[:, DL:].reshape(samples, HEADS, HD, lat_rows * lon_cols)
    query_heads = queries.reshape(Q, HEADS, HD)
    scores = jnp.einsum(
        "qhd,bhdn->bhqn", query_heads, key_heads, preferred_element_type=jnp.float32
    ) * HD ** (-0.5)
    maxima = jnp.max(scores, axis=-1)
    exponent = jnp.exp(scores - maxima[..., None])
    totals = jnp.sum(exponent, axis=-1)
    weights_bf = exponent.astype(jnp.bfloat16)
    weighted = jnp.einsum(
        "bhqn,bhdn->bqhd", weights_bf, value_heads, preferred_element_type=jnp.float32
    )
    return (block_features, maxima, totals, weighted.reshape(samples, Q, DL))


def rescale(weighted, factor):
    full_shape = weighted.shape
    heads_view = weighted.reshape(full_shape[0], full_shape[1], factor.shape[1], -1)
    return (heads_view * jnp.transpose(factor, (0, 2, 1))[..., None]).reshape(full_shape)


def normalize(weighted, totals):
    full_shape = weighted.shape
    heads_view = weighted.reshape(full_shape[0], full_shape[1], totals.shape[1], -1)
    return (heads_view / jnp.transpose(totals, (0, 2, 1))[..., None]).reshape(full_shape)


def combine_partial(earlier, later):
    highest = jnp.maximum(earlier[0], later[0])
    scale_one = jnp.exp(earlier[0] - highest)
    scale_two = jnp.exp(later[0] - highest)
    totals = earlier[1] * scale_one + later[1] * scale_two
    weighted = rescale(earlier[2], scale_one) + rescale(later[2], scale_two)
    return (highest, totals, weighted)


def per_device(fields, conv_weight, kv_weight, out_weight, norm_gain, queries):
    samples, channels, lat_rows, lon_cols = fields.shape
    widened = extended(fields, (("lon", 3),), 1, True)
    padded = extended(widened, (("lat", 2),), 1, False)
    block_count = lat_rows // BLK
    initial = (
        jnp.full((samples, HEADS, Q), -1e30, jnp.float32),
        jnp.zeros((samples, HEADS, Q), jnp.float32),
        jnp.zeros((samples, Q, DL), jnp.float32),
    )

    def scan_step(running_state, block_index):
        zero_index = jnp.zeros((), jnp.int32)
        window_in = lax.dynamic_slice(
            padded,
            (zero_index, zero_index, block_index * BLK, zero_index),
            (samples, channels, BLK + 2, lon_cols + 2),
        )
        block_features, maxima, totals, weighted = block_terms(
            window_in, conv_weight, kv_weight, queries, BLK, lon_cols
        )
        return (combine_partial(running_state, (maxima, totals, weighted)), block_features)

    running_state, feats = lax.scan(scan_step, initial, jnp.arange(block_count, dtype=jnp.int32))
    features = jnp.transpose(feats, (1, 2, 0, 3, 4)).reshape(
        samples, feats.shape[2], lat_rows, lon_cols
    )
    maxima, totals, weighted = running_state
    stats = jnp.concatenate([maxima, totals], axis=1)
    stats = jnp.transpose(stats, (0, 2, 1)).reshape(samples * Q, 2 * HEADS)
    stats = jnp.pad(stats, ((0, 0), (0, 120)))
    latents = reduce_all(weighted.reshape(samples * Q, DL), stats, out_weight, norm_gain)
    latents = latents.reshape(samples, Q, DL)
    return (features, latents)


def solution(mesh):
    in_specs = (P(None, None, "lat", "lon"), P(), P(), P(), P(), P())
    out_specs = (P(None, None, "lat", "lon"), P())
    return jax.shard_map(
        per_device, mesh=mesh, in_specs=in_specs, out_specs=out_specs, check_vma=False
    )
```

```python
import functools
import jax
import jax.numpy as jnp
from jax import lax
from jax.experimental import pallas as pl
from jax.experimental.pallas import tpu as pltpu
from jax.sharding import PartitionSpec as P

DL = 256
Q = 256
HEADS = 4
HD = 64
MESH = pl.DeviceIdType.MESH
ROWS = 8
NCHIP = 64


def reduce_kernel(
    w_ref, st_ref, ow_ref, gain_ref, out_ref,
    half_w, half_st, msg, recv, own, gath,
    sem_a, sem_b, sem_c,
):
    lat = lax.axis_index("lat")
    lon = lax.axis_index("lon")
    core = lax.rem(lon, 2)
    chip = lat * 16 + lon // 2
    partner = lon + 1 - 2 * core

    def peer(k):
        c = lax.rem(chip + k, NCHIP)
        return (c // 16, lax.rem(c, 16) * 2 + core)

    barrier = pltpu.get_barrier_semaphore()
    pl.semaphore_signal(barrier, inc=1, device_id=(lat, partner), device_id_type=MESH)

    def greet(k, _):
        pl.semaphore_signal(barrier, inc=1, device_id=peer(k), device_id_type=MESH)
        return 0

    lax.fori_loop(1, NCHIP, greet, 0)
    pl.semaphore_wait(barrier, NCHIP)

    give = 1 - core
    cw = pltpu.make_async_remote_copy(
        w_ref.at[give], half_w, sem_a.at[0], sem_a.at[1], device_id=(lat, partner), device_id_type=MESH)
    cs = pltpu.make_async_remote_copy(
        st_ref.at[give], half_st, sem_a.at[2], sem_a.at[3], device_id=(lat, partner), device_id_type=MESH)
    cs.start()
    cw.start()
    cs.wait()
    cw.wait()

    s1 = st_ref[core]
    s2 = half_st[...]
    peak = jnp.maximum(s1, s2)
    f1 = jnp.exp(s1 - peak)
    f2 = jnp.exp(s2 - peak)
    lane = lax.broadcasted_iota(jnp.int32, (512, 128), 1)
    t1 = pltpu.roll(s1, 124, 1)
    t2 = pltpu.roll(s2, 124, 1)
    tot = t1 * f1 + t2 * f2
    for h in range(4):
        cols = slice(h * 64, h * 64 + 64)
        val = w_ref[core, :, cols] * f1[:, h:h + 1] + half_w[:, cols] * f2[:, h:h + 1]
        msg[:, :, cols] = val.reshape(NCHIP, ROWS, 64).astype(jnp.bfloat16)

    def limbs(v):
        a = v.astype(jnp.bfloat16).astype(jnp.float32)
        b = (v - a).astype(jnp.bfloat16).astype(jnp.float32)
        return a, b, v - a - b

    m0, m1, m2 = limbs(jnp.where(lane < 4, peak, 0.0))
    q0, q1, q2 = limbs(jnp.where(lane < 4, tot, 0.0))
    packed = (m0 + pltpu.roll(m1, 4, 1) + pltpu.roll(m2, 8, 1)
              + pltpu.roll(q0, 12, 1) + pltpu.roll(q1, 16, 1) + pltpu.roll(q2, 20, 1))
    msg[:, :, 256:384] = packed.reshape(NCHIP, ROWS, 128).astype(jnp.bfloat16)

    def scatter(k, _):
        c = lax.rem(chip + k, NCHIP)
        pltpu.make_async_remote_copy(
            msg.at[c], recv.at[k - 1], sem_b.at[0], sem_b.at[1], device_id=peer(k), device_id_type=MESH).start()
        return 0

    lax.fori_loop(1, NCHIP, scatter, 0)
    own[...] = msg[chip]
    pltpu.make_async_copy(recv, recv, sem_b.at[1]).wait()

    def stats(v):
        m = v + pltpu.roll(v, 124, 1) + pltpu.roll(v, 120, 1)
        t = pltpu.roll(v, 116, 1) + pltpu.roll(v, 112, 1) + pltpu.roll(v, 108, 1)
        return m, t

    def unpack(buf):
        return buf.astype(jnp.float32)

    all_st = jnp.concatenate([recv[:, :, 256:384].astype(jnp.float32), own[:, 256:384].astype(jnp.float32)[None]], axis=0)
    am, at = stats(all_st.reshape(512, 128))
    am = am.reshape(NCHIP, ROWS, 128)
    at = at.reshape(NCHIP, ROWS, 128)
    top = jnp.max(am, axis=0)
    fac = jnp.exp(am - top[None])
    total = jnp.sum(fac * at, axis=0)
    for h in range(4):
        cols = slice(h * 64, h * 64 + 64)
        acc = (jnp.sum(recv[:, :, cols].astype(jnp.float32) * fac[:63, :, h:h + 1], axis=0)
               + own[:, cols].astype(jnp.float32) * fac[63, :, h:h + 1])
        gath[core * NCHIP + chip, :, cols] = (acc / total[:, h:h + 1]).astype(jnp.bfloat16)
    pltpu.make_async_copy(recv, recv, sem_b.at[0]).wait()

    mine = core * NCHIP + chip

    def spread(k, _):
        pltpu.make_async_remote_copy(
            gath.at[mine], gath.at[mine], sem_c.at[0], sem_c.at[1], device_id=peer(k), device_id_type=MESH).start()
        return 0

    lax.fori_loop(1, NCHIP, spread, 0)
    size = gath.at[pl.ds(0, NCHIP - 1)]
    pltpu.make_async_copy(size, size, sem_c.at[1]).wait()
    pltpu.make_async_copy(size, size, sem_c.at[0]).wait()
    block = gath.at[pl.ds(core * NCHIP, NCHIP)]
    cg = pltpu.make_async_remote_copy(
        block, block, sem_c.at[2], sem_c.at[3], device_id=(lat, partner), device_id_type=MESH)
    cg.start()
    cg.wait()
    att = gath[...].astype(jnp.float32).reshape(1024, 256).astype(jnp.bfloat16)
    proj = jnp.dot(att, ow_ref[...], preferred_element_type=jnp.float32)
    out_ref[...] = (
        proj * lax.rsqrt(jnp.mean(proj * proj, axis=-1, keepdims=True) + 1e-06) * gain_ref[...]
    )


def reduce_all(weighted, stats, out_weight, norm_gain):
    vm = pl.BlockSpec(memory_space=pltpu.VMEM)
    return pl.pallas_call(
        reduce_kernel,
        out_shape=jax.ShapeDtypeStruct((1024, 256), jnp.float32),
        in_specs=[vm] * 4,
        out_specs=vm,
        scratch_shapes=[
            pltpu.VMEM((512, 256), jnp.float32),
            pltpu.VMEM((512, 128), jnp.float32),
            pltpu.VMEM((NCHIP, ROWS, 384), jnp.bfloat16),
            pltpu.VMEM((NCHIP - 1, ROWS, 384), jnp.bfloat16),
            pltpu.VMEM((ROWS, 384), jnp.bfloat16),
            pltpu.VMEM((2 * NCHIP, ROWS, 256), jnp.bfloat16),
            pltpu.SemaphoreType.DMA((4,)),
            pltpu.SemaphoreType.DMA((2,)),
            pltpu.SemaphoreType.DMA((4,)),
        ],
        compiler_params=pltpu.CompilerParams(
            collective_id=1, has_side_effects=True, vmem_limit_bytes=32 * 1024 * 1024
        ),
    )(weighted.reshape(2, 512, 256), stats.reshape(2, 512, 128), out_weight, norm_gain.reshape(1, 256))


CP = 80
KROW = 3 * CP
SCALE = HD ** (-0.5)
NT = (((1,), (1,)), ((), ()))


def halo_kernel(
    xt_ref, cw_ref, kv_ref, rows_ref, cols_ref, w2_ref, kv2_ref,
    edge, got, taps, send_sem, recv_sem,
):
    lat = lax.axis_index("lat")
    lon = lax.axis_index("lon")
    nlat = lax.axis_size("lat")
    nlon = lax.axis_size("lon")
    right = lax.rem(lon + 1, nlon)
    left = lax.rem(lon + nlon - 1, nlon)
    barrier = pltpu.get_barrier_semaphore()

    def greet(dlat, dlon):
        pl.semaphore_signal(barrier, inc=1, device_id=(dlat, dlon), device_id_type=MESH)

    greet(lat, left)
    greet(lat, right)

    @pl.when(lat > 0)
    def _():
        greet(lat - 1, left)
        greet(lat - 1, lon)
        greet(lat - 1, right)

    @pl.when(lat < nlat - 1)
    def _():
        greet(lat + 1, left)
        greet(lat + 1, lon)
        greet(lat + 1, right)

    lane = lax.broadcasted_iota(jnp.int32, (CP, 128), 1)
    last = jnp.zeros((CP, 128), jnp.float32)
    first = jnp.zeros((CP, 128), jnp.float32)
    for b in range(xt_ref.shape[0]):
        for i in range(24):
            at = b * 24 + i
            row = xt_ref[b, i].astype(jnp.float32)
            last = jnp.where(lane == at, pltpu.roll(row, (at + 1) % 128, 1), last)
            first = jnp.where(lane == at, pltpu.roll(row, at, 1), first)
    edge[0] = last.astype(jnp.bfloat16)
    edge[1] = first.astype(jnp.bfloat16)

    def copy(src, dst, n, dlat, dlon):
        return pltpu.make_async_remote_copy(
            src, dst, send_sem.at[n], recv_sem.at[n], device_id=(dlat, dlon), device_id_type=MESH)

    same = [
        copy(edge.at[0], got.at[0, 0], 0, lat, right),
        copy(edge.at[1], got.at[1, 0], 1, lat, left),
    ]
    down = [
        copy(xt_ref.at[:, 23], rows_ref.at[0], 2, lat + 1, lon),
        copy(edge.at[0], got.at[0, 1], 3, lat + 1, right),
        copy(edge.at[1], got.at[1, 1], 4, lat + 1, left),
    ]
    up = [
        copy(xt_ref.at[:, 0], rows_ref.at[1], 5, lat - 1, lon),
        copy(edge.at[0], got.at[0, 2], 6, lat - 1, right),
        copy(edge.at[1], got.at[1, 2], 7, lat - 1, left),
    ]
    inner = jnp.logical_and(lat > 0, lat < nlat - 1)

    @pl.when(inner)
    def _():
        pl.semaphore_wait(barrier, 8)

    @pl.when(jnp.logical_not(inner))
    def _():
        pl.semaphore_wait(barrier, 5)

    for c in same:
        c.start()

    @pl.when(lat < nlat - 1)
    def _():
        for c in down:
            c.start()

    @pl.when(lat > 0)
    def _():
        for c in up:
            c.start()

    taps[...] = jnp.zeros_like(taps)
    for t in range(9):
        value = cw_ref[t].astype(jnp.float32)
        value = jnp.concatenate([value, jnp.zeros((CP - value.shape[0], 128), jnp.float32)], axis=0).astype(jnp.bfloat16)
        taps[t * CP:(t + 1) * CP, 0:128] = value
        taps[KROW + t * CP:KROW + (t + 1) * CP, 128:256] = value
    out_at = lax.broadcasted_iota(jnp.int32, (256, 256), 0)
    in_at = lax.broadcasted_iota(jnp.int32, (256, 256), 1)
    spread = jnp.where(out_at == jnp.where(in_at < 128, 2 * in_at, 2 * in_at - 255), 1.0, 0.0).astype(jnp.bfloat16)
    w2_ref[...] = lax.dot_general(spread, taps[...], NT, preferred_element_type=jnp.float32).astype(jnp.bfloat16)
    for r in range(2):
        kv2_ref[r * 512:(r + 1) * 512] = lax.dot_general(
            kv_ref[...], spread[:, r * 128:(r + 1) * 128], NT, preferred_element_type=jnp.float32).astype(jnp.bfloat16)

    for c in same:
        c.wait()

    @pl.when(lat > 0)
    def _():
        for c in down:
            c.wait_recv()
        for c in up:
            c.wait_send()

    @pl.when(lat < nlat - 1)
    def _():
        for c in up:
            c.wait_recv()
        for c in down:
            c.wait_send()

    @pl.when(lat == 0)
    def _():
        rows_ref[0] = jnp.zeros_like(rows_ref[0])
        for side in range(2):
            got[side, 1] = jnp.zeros((CP, 128), jnp.bfloat16)

    @pl.when(lat == nlat - 1)
    def _():
        rows_ref[1] = jnp.zeros_like(rows_ref[1])
        for side in range(2):
            got[side, 2] = jnp.zeros((CP, 128), jnp.bfloat16)

    for side in range(2):
        mid = got[side, 0].astype(jnp.float32)
        above = got[side, 1].astype(jnp.float32)
        below = got[side, 2].astype(jnp.float32)
        for b in range(4):
            value = pltpu.roll(mid, (129 - b * 24) % 128, 1)
            value = jnp.where(lane == 0, pltpu.roll(above, (128 - b * 24 - 23) % 128, 1), value)
            value = jnp.where(lane == 25, pltpu.roll(below, (128 + 25 - b * 24) % 128, 1), value)
            cols_ref[side, b] = value.astype(jnp.bfloat16)


def halo(xt, conv_t, kv_weight):
    vm = pl.BlockSpec(memory_space=pltpu.VMEM)
    samples = xt.shape[0]
    return pl.pallas_call(
        halo_kernel,
        out_shape=(
            jax.ShapeDtypeStruct((2, samples, CP, 128), jnp.bfloat16),
            jax.ShapeDtypeStruct((2, samples, CP, 128), jnp.bfloat16),
            jax.ShapeDtypeStruct((256, 4 * KROW), jnp.bfloat16),
            jax.ShapeDtypeStruct((1024, 256), jnp.bfloat16),
        ),
        in_specs=[vm] * 3,
        out_specs=(vm,) * 4,
        scratch_shapes=[
            pltpu.VMEM((2, CP, 128), jnp.bfloat16),
            pltpu.VMEM((2, 3, CP, 128), jnp.bfloat16),
            pltpu.VMEM((4 * KROW, 256), jnp.bfloat16),
            pltpu.SemaphoreType.DMA((8,)),
            pltpu.SemaphoreType.DMA((8,)),
        ],
        compiler_params=pltpu.CompilerParams(
            collective_id=0, has_side_effects=True, vmem_limit_bytes=32 * 1024 * 1024),
    )(xt, conv_t, kv_weight)


def encode_kernel(
    xt_ref, rows_ref, cols_ref, w2_ref, kv2_ref, q_ref, feat_ref, w_out, st_out,
    x3, qs, kvs, run,
):
    chunk = pl.program_id(1)
    lane = lax.broadcasted_iota(jnp.int32, (CP, 128), 1)

    @pl.when(chunk == 0)
    def _():
        for h in range(HEADS):
            qs[h] = (q_ref[:, h * HD:(h + 1) * HD].astype(jnp.float32) * SCALE).astype(jnp.bfloat16)
        lo = cols_ref[0, 0].astype(jnp.float32)
        hi = cols_ref[1, 0].astype(jnp.float32)
        for i in range(26):
            row = rows_ref[0, 0] if i == 0 else rows_ref[1, 0] if i == 25 else xt_ref[0, i - 1]
            wide = row.astype(jnp.float32)
            before = jnp.where(lane == 0, pltpu.roll(lo, (128 - i) % 128, 1), pltpu.roll(wide, 1, 1))
            after = jnp.where(lane == 127, pltpu.roll(hi, 127 - i, 1), pltpu.roll(wide, 127, 1))
            x3[i, 0:CP] = before.astype(jnp.bfloat16)
            x3[i, CP:2 * CP] = row
            x3[i, 2 * CP:3 * CP] = after.astype(jnp.bfloat16)

    w2 = w2_ref[...]
    for g in range(2):
        base = chunk * 8 + g * 4
        one = x3[pl.ds(base, 4)].reshape(4 * KROW, 128)
        two = x3[pl.ds(base + 2, 4)].reshape(4 * KROW, 128)
        both = jnp.concatenate([one, two], axis=1)
        conv = jnp.dot(w2, both, preferred_element_type=jnp.float32)
        feats = jax.nn.gelu(conv, approximate=True).astype(jnp.bfloat16)
        feat_ref[0, :, 2 * g] = feats[:, 0:128].reshape(128, 2, 128)
        feat_ref[0, :, 2 * g + 1] = feats[:, 128:256].reshape(128, 2, 128)
        kvs[:, g * 256:(g + 1) * 256] = jnp.dot(
            kv2_ref[...], feats, preferred_element_type=jnp.float32).astype(jnp.bfloat16)

    st_lane = lax.broadcasted_iota(jnp.int32, (256, 128), 1)
    old = jnp.where(chunk == 0, jnp.where(st_lane < 4, -3e38, 0.0), run[...])
    new = jnp.zeros((256, 128), jnp.float32)
    for h in range(HEADS):
        rows = slice(h * HD, (h + 1) * HD)
        s0 = jnp.dot(qs[h], kvs[rows], preferred_element_type=jnp.float32)
        s1 = jnp.dot(qs[h], kvs[512 + h * HD:512 + (h + 1) * HD], preferred_element_type=jnp.float32)
        top = jnp.max(jnp.maximum(s0, s1), axis=1, keepdims=True)
        before = old[:, h:h + 1]
        peak = jnp.maximum(before, top)
        mine = jnp.exp(top - peak)
        keep = jnp.exp(before - peak)
        p0 = jnp.exp(s0 - top)
        p1 = jnp.exp(s1 - top)
        total = jnp.sum(p0 + p1, axis=1, keepdims=True)
        v0 = kvs[256 + h * HD:256 + (h + 1) * HD]
        v1 = kvs[768 + h * HD:768 + (h + 1) * HD]
        part = (lax.dot_general(p0.astype(jnp.bfloat16), v0, NT, preferred_element_type=jnp.float32)
                + lax.dot_general(p1.astype(jnp.bfloat16), v1, NT, preferred_element_type=jnp.float32))
        sofar = jnp.where(chunk == 0, 0.0, w_out[0, :, rows])
        w_out[0, :, rows] = sofar * keep + part * mine
        total = old[:, 4 + h:5 + h] * keep + total * mine
        new = jnp.where(st_lane == h, peak, jnp.where(st_lane == 4 + h, total, new))
    run[...] = new
    st_out[0] = new


def encode(xt, rows, cols, w2, kv2, queries):
    samples = xt.shape[0]
    whole = pl.BlockSpec(memory_space=pltpu.VMEM)
    side = pl.BlockSpec((2, 1, CP, 128), lambda b, c: (0, b, 0, 0))
    return pl.pallas_call(
        encode_kernel,
        grid=(samples, 3),
        out_shape=(
            jax.ShapeDtypeStruct((samples, 128, 12, 2, 128), jnp.bfloat16),
            jax.ShapeDtypeStruct((samples, Q, DL), jnp.float32),
            jax.ShapeDtypeStruct((samples, Q, 128), jnp.float32),
        ),
        in_specs=[
            pl.BlockSpec((1, 24, CP, 128), lambda b, c: (b, 0, 0, 0)),
            side, side, whole, whole, whole,
        ],
        out_specs=(
            pl.BlockSpec((1, 128, 4, 2, 128), lambda b, c: (b, 0, c, 0, 0)),
            pl.BlockSpec((1, Q, DL), lambda b, c: (b, 0, 0)),
            pl.BlockSpec((1, Q, 128), lambda b, c: (b, 0, 0)),
        ),
        scratch_shapes=[
            pltpu.VMEM((26, KROW, 128), jnp.bfloat16),
            pltpu.VMEM((HEADS, Q, HD), jnp.bfloat16),
            pltpu.VMEM((1024, 512), jnp.bfloat16),
            pltpu.VMEM((Q, 128), jnp.float32),
        ],
        compiler_params=pltpu.CompilerParams(
            dimension_semantics=("arbitrary", "arbitrary"), vmem_limit_bytes=48 * 1024 * 1024),
    )(xt, rows, cols, w2, kv2, queries)


def per_device(fields, conv_weight, kv_weight, out_weight, norm_gain, queries):
    samples, channels, lat_rows, lon_cols = fields.shape
    xt = jnp.pad(jnp.transpose(fields, (0, 2, 1, 3)), ((0, 0), (0, 0), (0, CP - channels), (0, 0)))
    conv_t = jnp.transpose(conv_weight, (0, 2, 1))
    rows, cols, w2, kv2 = halo(xt, conv_t, kv_weight)
    feats, weighted, stats = encode(xt, rows, cols, w2, kv2, queries)
    features = feats.reshape(samples, 128, lat_rows, lon_cols)
    latents = reduce_all(weighted, stats, out_weight, norm_gain)
    return (features, latents.reshape(samples, Q, DL))


def solution(mesh):
    in_specs = (P(None, None, "lat", "lon"), P(), P(), P(), P(), P())
    out_specs = (P(None, None, "lat", "lon"), P())
    return jax.shard_map(
        per_device, mesh=mesh, in_specs=in_specs, out_specs=out_specs, check_vma=False
    )
```

```python
import functools
import jax
import jax.numpy as jnp
from jax import lax
from jax.experimental import pallas as pl
from jax.experimental.pallas import tpu as pltpu
from jax.sharding import PartitionSpec as P

DL = 256
Q = 256
HEADS = 4
HD = 64
MESH = pl.DeviceIdType.MESH
ROWS = 8
NCHIP = 64


def reduce_kernel(
    w_ref, st_ref, ow_ref, gain_ref, out_ref,
    half_w, half_st, msg, recv, own, gath,
    sem_a, sem_b, sem_c,
):
    lat = lax.axis_index("lat")
    lon = lax.axis_index("lon")
    core = lax.rem(lon, 2)
    chip = lat * 16 + lon // 2
    partner = lon + 1 - 2 * core

    def peer(k):
        c = lax.rem(chip + k, NCHIP)
        return (c // 16, lax.rem(c, 16) * 2 + core)

    barrier = pltpu.get_barrier_semaphore()
    pl.semaphore_signal(barrier, inc=1, device_id=(lat, partner), device_id_type=MESH)

    def greet(k, _):
        pl.semaphore_signal(barrier, inc=1, device_id=peer(k), device_id_type=MESH)
        return 0

    lax.fori_loop(1, NCHIP, greet, 0)
    pl.semaphore_wait(barrier, NCHIP)

    give = 1 - core
    cw = pltpu.make_async_remote_copy(
        w_ref.at[give], half_w, sem_a.at[0], sem_a.at[1], device_id=(lat, partner), device_id_type=MESH)
    cs = pltpu.make_async_remote_copy(
        st_ref.at[give], half_st, sem_a.at[2], sem_a.at[3], device_id=(lat, partner), device_id_type=MESH)
    cs.start()
    cw.start()
    cs.wait()
    cw.wait()

    s1 = st_ref[core]
    s2 = half_st[...]
    peak = jnp.maximum(s1, s2)
    f1 = jnp.exp(s1 - peak)
    f2 = jnp.exp(s2 - peak)
    lane = lax.broadcasted_iota(jnp.int32, (512, 128), 1)
    t1 = pltpu.roll(s1, 124, 1)
    t2 = pltpu.roll(s2, 124, 1)
    tot = t1 * f1 + t2 * f2
    for h in range(4):
        cols = slice(h * 64, h * 64 + 64)
        val = w_ref[core, :, cols] * f1[:, h:h + 1] + half_w[:, cols] * f2[:, h:h + 1]
        msg[:, :, cols] = val.reshape(NCHIP, ROWS, 64).astype(jnp.bfloat16)

    def limbs(v):
        a = v.astype(jnp.bfloat16).astype(jnp.float32)
        b = (v - a).astype(jnp.bfloat16).astype(jnp.float32)
        return a, b, v - a - b

    m0, m1, m2 = limbs(jnp.where(lane < 4, peak, 0.0))
    q0, q1, q2 = limbs(jnp.where(lane < 4, tot, 0.0))
    packed = (m0 + pltpu.roll(m1, 4, 1) + pltpu.roll(m2, 8, 1)
              + pltpu.roll(q0, 12, 1) + pltpu.roll(q1, 16, 1) + pltpu.roll(q2, 20, 1))
    msg[:, :, 256:384] = packed.reshape(NCHIP, ROWS, 128).astype(jnp.bfloat16)

    def scatter(k, _):
        c = lax.rem(chip + k, NCHIP)
        pltpu.make_async_remote_copy(
            msg.at[c], recv.at[k - 1], sem_b.at[0], sem_b.at[1], device_id=peer(k), device_id_type=MESH).start()
        return 0

    lax.fori_loop(1, NCHIP, scatter, 0)
    own[...] = msg[chip]
    pltpu.make_async_copy(recv, recv, sem_b.at[1]).wait()

    def stats(v):
        m = v + pltpu.roll(v, 124, 1) + pltpu.roll(v, 120, 1)
        t = pltpu.roll(v, 116, 1) + pltpu.roll(v, 112, 1) + pltpu.roll(v, 108, 1)
        return m, t

    def unpack(buf):
        return buf.astype(jnp.float32)

    all_st = jnp.concatenate([recv[:, :, 256:384].astype(jnp.float32), own[:, 256:384].astype(jnp.float32)[None]], axis=0)
    am, at = stats(all_st.reshape(512, 128))
    am = am.reshape(NCHIP, ROWS, 128)
    at = at.reshape(NCHIP, ROWS, 128)
    top = jnp.max(am, axis=0)
    fac = jnp.exp(am - top[None])
    total = jnp.sum(fac * at, axis=0)
    for h in range(4):
        cols = slice(h * 64, h * 64 + 64)
        acc = (jnp.sum(recv[:, :, cols].astype(jnp.float32) * fac[:63, :, h:h + 1], axis=0)
               + own[:, cols].astype(jnp.float32) * fac[63, :, h:h + 1])
        gath[core * NCHIP + chip, :, cols] = (acc / total[:, h:h + 1]).astype(jnp.bfloat16)
    pltpu.make_async_copy(recv, recv, sem_b.at[0]).wait()

    mine = core * NCHIP + chip

    def spread(k, _):
        pltpu.make_async_remote_copy(
            gath.at[mine], gath.at[mine], sem_c.at[0], sem_c.at[1], device_id=peer(k), device_id_type=MESH).start()
        return 0

    lax.fori_loop(1, NCHIP, spread, 0)
    size = gath.at[pl.ds(0, NCHIP - 1)]
    pltpu.make_async_copy(size, size, sem_c.at[1]).wait()
    pltpu.make_async_copy(size, size, sem_c.at[0]).wait()
    block = gath.at[pl.ds(core * NCHIP, NCHIP)]
    cg = pltpu.make_async_remote_copy(
        block, block, sem_c.at[2], sem_c.at[3], device_id=(lat, partner), device_id_type=MESH)
    cg.start()
    cg.wait()
    att = gath[...].astype(jnp.float32).reshape(1024, 256).astype(jnp.bfloat16)
    proj = jnp.dot(att, ow_ref[...], preferred_element_type=jnp.float32)
    out_ref[...] = (
        proj * lax.rsqrt(jnp.mean(proj * proj, axis=-1, keepdims=True) + 1e-06) * gain_ref[...]
    )


def reduce_all(weighted, stats, out_weight, norm_gain):
    vm = pl.BlockSpec(memory_space=pltpu.VMEM)
    return pl.pallas_call(
        reduce_kernel,
        out_shape=jax.ShapeDtypeStruct((1024, 256), jnp.float32),
        in_specs=[vm] * 4,
        out_specs=vm,
        scratch_shapes=[
            pltpu.VMEM((512, 256), jnp.float32),
            pltpu.VMEM((512, 128), jnp.float32),
            pltpu.VMEM((NCHIP, ROWS, 384), jnp.bfloat16),
            pltpu.VMEM((NCHIP - 1, ROWS, 384), jnp.bfloat16),
            pltpu.VMEM((ROWS, 384), jnp.bfloat16),
            pltpu.VMEM((2 * NCHIP, ROWS, 256), jnp.bfloat16),
            pltpu.SemaphoreType.DMA((4,)),
            pltpu.SemaphoreType.DMA((2,)),
            pltpu.SemaphoreType.DMA((4,)),
        ],
        compiler_params=pltpu.CompilerParams(
            collective_id=1, has_side_effects=True, vmem_limit_bytes=32 * 1024 * 1024
        ),
    )(weighted.reshape(2, 512, 256), stats.reshape(2, 512, 128), out_weight, norm_gain.reshape(1, 256))


CP = 80
KROW = 3 * CP
SCALE = HD ** (-0.5)
NT = (((1,), (1,)), ((), ()))


def halo_kernel(
    xt_ref, cw_ref, kv_ref, rows_ref, cols_ref, w2_ref, kt_ref, vt_ref,
    edge, got, taps, send_sem, recv_sem,
):
    lat = lax.axis_index("lat")
    lon = lax.axis_index("lon")
    nlat = lax.axis_size("lat")
    nlon = lax.axis_size("lon")
    right = lax.rem(lon + 1, nlon)
    left = lax.rem(lon + nlon - 1, nlon)
    barrier = pltpu.get_barrier_semaphore()

    def greet(dlat, dlon):
        pl.semaphore_signal(barrier, inc=1, device_id=(dlat, dlon), device_id_type=MESH)

    greet(lat, left)
    greet(lat, right)

    @pl.when(lat > 0)
    def _():
        greet(lat - 1, left)
        greet(lat - 1, lon)
        greet(lat - 1, right)

    @pl.when(lat < nlat - 1)
    def _():
        greet(lat + 1, left)
        greet(lat + 1, lon)
        greet(lat + 1, right)

    lane = lax.broadcasted_iota(jnp.int32, (CP, 128), 1)
    last = jnp.zeros((CP, 128), jnp.float32)
    first = jnp.zeros((CP, 128), jnp.float32)
    for b in range(xt_ref.shape[0]):
        for i in range(24):
            at = b * 24 + i
            row = xt_ref[b, i].astype(jnp.float32)
            last = jnp.where(lane == at, pltpu.roll(row, (at + 1) % 128, 1), last)
            first = jnp.where(lane == at, pltpu.roll(row, at, 1), first)
    edge[0] = last.astype(jnp.bfloat16)
    edge[1] = first.astype(jnp.bfloat16)

    def copy(src, dst, n, dlat, dlon):
        return pltpu.make_async_remote_copy(
            src, dst, send_sem.at[n], recv_sem.at[n], device_id=(dlat, dlon), device_id_type=MESH)

    same = [
        copy(edge.at[0], got.at[0, 0], 0, lat, right),
        copy(edge.at[1], got.at[1, 0], 1, lat, left),
    ]
    down = [
        copy(xt_ref.at[:, 23], rows_ref.at[0], 2, lat + 1, lon),
        copy(edge.at[0], got.at[0, 1], 3, lat + 1, right),
        copy(edge.at[1], got.at[1, 1], 4, lat + 1, left),
    ]
    up = [
        copy(xt_ref.at[:, 0], rows_ref.at[1], 5, lat - 1, lon),
        copy(edge.at[0], got.at[0, 2], 6, lat - 1, right),
        copy(edge.at[1], got.at[1, 2], 7, lat - 1, left),
    ]
    inner = jnp.logical_and(lat > 0, lat < nlat - 1)

    @pl.when(inner)
    def _():
        pl.semaphore_wait(barrier, 8)

    @pl.when(jnp.logical_not(inner))
    def _():
        pl.semaphore_wait(barrier, 5)

    for c in same:
        c.start()

    @pl.when(lat < nlat - 1)
    def _():
        for c in down:
            c.start()

    @pl.when(lat > 0)
    def _():
        for c in up:
            c.start()

    taps[...] = jnp.zeros_like(taps)
    for t in range(9):
        value = cw_ref[t].astype(jnp.float32)
        value = jnp.concatenate([value, jnp.zeros((CP - value.shape[0], 128), jnp.float32)], axis=0).astype(jnp.bfloat16)
        taps[t * CP:(t + 1) * CP, 0:128] = value
        taps[KROW + t * CP:KROW + (t + 1) * CP, 128:256] = value
    out_at = lax.broadcasted_iota(jnp.int32, (256, 256), 0)
    in_at = lax.broadcasted_iota(jnp.int32, (256, 256), 1)
    spread = jnp.where(out_at == jnp.where(in_at < 128, 2 * in_at, 2 * in_at - 255), 1.0, 0.0).astype(jnp.bfloat16)
    w2_ref[...] = lax.dot_general(spread, taps[...], NT, preferred_element_type=jnp.float32).astype(jnp.bfloat16)
    for r in range(2):
        some = spread[:, r * 128:(r + 1) * 128]
        kt_ref[:, r * DL:(r + 1) * DL] = lax.dot_general(
            some, kv_ref[0:DL], NT, preferred_element_type=jnp.float32).astype(jnp.bfloat16)
        vt_ref[r * DL:(r + 1) * DL] = lax.dot_general(
            kv_ref[DL:2 * DL], some, NT, preferred_element_type=jnp.float32).astype(jnp.bfloat16)

    for c in same:
        c.wait()

    @pl.when(lat > 0)
    def _():
        for c in down:
            c.wait_recv()
        for c in up:
            c.wait_send()

    @pl.when(lat < nlat - 1)
    def _():
        for c in up:
            c.wait_recv()
        for c in down:
            c.wait_send()

    @pl.when(lat == 0)
    def _():
        rows_ref[0] = jnp.zeros_like(rows_ref[0])
        for side in range(2):
            got[side, 1] = jnp.zeros((CP, 128), jnp.bfloat16)

    @pl.when(lat == nlat - 1)
    def _():
        rows_ref[1] = jnp.zeros_like(rows_ref[1])
        for side in range(2):
            got[side, 2] = jnp.zeros((CP, 128), jnp.bfloat16)

    for side in range(2):
        mid = got[side, 0].astype(jnp.float32)
        above = got[side, 1].astype(jnp.float32)
        below = got[side, 2].astype(jnp.float32)
        for b in range(4):
            value = pltpu.roll(mid, (129 - b * 24) % 128, 1)
            value = jnp.where(lane == 0, pltpu.roll(above, (128 - b * 24 - 23) % 128, 1), value)
            value = jnp.where(lane == 25, pltpu.roll(below, (128 + 25 - b * 24) % 128, 1), value)
            cols_ref[side, b] = value.astype(jnp.bfloat16)


def halo(xt, conv_t, kv_weight):
    vm = pl.BlockSpec(memory_space=pltpu.VMEM)
    samples = xt.shape[0]
    return pl.pallas_call(
        halo_kernel,
        out_shape=(
            jax.ShapeDtypeStruct((2, samples, CP, 128), jnp.bfloat16),
            jax.ShapeDtypeStruct((2, samples, CP, 128), jnp.bfloat16),
            jax.ShapeDtypeStruct((256, 4 * KROW), jnp.bfloat16),
            jax.ShapeDtypeStruct((256, 512), jnp.bfloat16),
            jax.ShapeDtypeStruct((512, 256), jnp.bfloat16),
        ),
        in_specs=[vm] * 3,
        out_specs=(vm,) * 5,
        scratch_shapes=[
            pltpu.VMEM((2, CP, 128), jnp.bfloat16),
            pltpu.VMEM((2, 3, CP, 128), jnp.bfloat16),
            pltpu.VMEM((4 * KROW, 256), jnp.bfloat16),
            pltpu.SemaphoreType.DMA((8,)),
            pltpu.SemaphoreType.DMA((8,)),
        ],
        compiler_params=pltpu.CompilerParams(
            collective_id=0, has_side_effects=True, vmem_limit_bytes=32 * 1024 * 1024),
    )(xt, conv_t, kv_weight)


NBLK = 12
TILE = 512


def encode_kernel(
    xt_ref, rows_ref, cols_ref, w2_ref, kt_ref, vt_ref, q_ref, feat_ref, w_out, st_out,
    x3, qs, k_a, k_b, v_a, v_b, feat_a, feat_b, refs, tot, acc, psums, parts, sem,
):
    step = pl.program_id(0)
    ks = (k_a, k_b)
    vs = (v_a, v_b)
    fbuf = (feat_a, feat_b)
    lane = lax.broadcasted_iota(jnp.int32, (CP, 128), 1)

    @pl.when(step == 0)
    def _():
        turned = (q_ref[...].astype(jnp.float32) * SCALE).T
        owner = lax.broadcasted_iota(jnp.int32, (DL, Q), 0) // HD
        for h in range(HEADS):
            qs[h] = jnp.where(owner == h, turned, 0.0).astype(jnp.bfloat16)

    def shifted(b):
        lo = cols_ref[0, b].astype(jnp.float32)
        hi = cols_ref[1, b].astype(jnp.float32)
        for i in range(26):
            row = rows_ref[0, b] if i == 0 else rows_ref[1, b] if i == 25 else xt_ref[b, i - 1]
            wide = row.astype(jnp.float32)
            before = jnp.where(lane == 0, pltpu.roll(lo, (128 - i) % 128, 1), pltpu.roll(wide, 1, 1))
            after = jnp.where(lane == 127, pltpu.roll(hi, 127 - i, 1), pltpu.roll(wide, 127, 1))
            x3[i, 0:CP] = before.astype(jnp.bfloat16)
            x3[i, CP:2 * CP] = row
            x3[i, 2 * CP:3 * CP] = after.astype(jnp.bfloat16)

    def out_copy(n, slot):
        return pltpu.make_async_copy(
            fbuf[slot], feat_ref.at[n // 3, :, pl.ds(lax.rem(n, 3) * 4, 4)], sem.at[slot])

    def conv_of(c, g):
        base = c * 8 + g * 4
        one = x3[pl.ds(base, 4)].reshape(4 * KROW, 128)
        two = x3[pl.ds(base + 2, 4)].reshape(4 * KROW, 128)
        both = jnp.concatenate([one, two], axis=1)
        conv = jnp.dot(w2_ref[...], both, preferred_element_type=jnp.float32)
        return jax.nn.gelu(conv, approximate=True).astype(jnp.bfloat16)

    def keep_features(feats, slot, g):
        fbuf[slot][:, 2 * g] = feats[:, 0:128].reshape(128, 2, 128)
        fbuf[slot][:, 2 * g + 1] = feats[:, 128:256].reshape(128, 2, 128)

    def project(feats, slot, g):
        turned = feats.T
        values = jnp.dot(vt_ref[...], feats, preferred_element_type=jnp.float32).astype(jnp.bfloat16)
        keys = jnp.dot(turned, kt_ref[...], preferred_element_type=jnp.float32).astype(jnp.bfloat16)
        for r in range(2):
            at = r * 512 + g * 256
            vs[slot][:, at:at + 256] = values[r * DL:(r + 1) * DL]
            ks[slot][at:at + 256] = keys[:, r * DL:(r + 1) * DL]

    def weigh(slot, h, ref, psum, part):
        for n in range(0, 1024, TILE):
            s = jnp.dot(ks[slot][n:n + TILE], qs[h], preferred_element_type=jnp.float32)
            p = jnp.exp(s - ref)
            psum = psum + jnp.sum(p.reshape(TILE // 8, 8, Q), axis=0)
            part = part + jnp.dot(
                vs[slot][h * HD:(h + 1) * HD, n:n + TILE], p.astype(jnp.bfloat16), preferred_element_type=jnp.float32)
        return psum, part

    def score(slot, h, n):
        return jnp.dot(ks[slot][n:n + TILE], qs[h], preferred_element_type=jnp.float32)

    def absorb(slot, state, s, h, n):
        p = jnp.exp(s - refs[h])
        psum = jnp.sum(p.reshape(TILE // 8, 8, Q), axis=0)
        part = jnp.dot(
            vs[slot][h * HD:(h + 1) * HD, n:n + TILE], p.astype(jnp.bfloat16), preferred_element_type=jnp.float32)
        if n > 0:
            psum = psum + state[h][0]
            part = part + state[h][1]
        state[h] = (psum, part)
        if n + TILE == 1024:
            psums[h] = psum
            parts[h] = part

    def head(slot, h):
        psum, part = weigh(slot, h, refs[h], jnp.zeros((8, Q), jnp.float32), jnp.zeros((HD, Q), jnp.float32))
        psums[h] = psum
        parts[h] = part

    def restart(slot):
        for h in range(HEADS):
            s = jnp.dot(ks[slot][0:128], qs[h], preferred_element_type=jnp.float32)
            refs[h] = jnp.max(s, axis=0, keepdims=True)
            tot[h] = jnp.zeros((8, Q), jnp.float32)
            acc[h] = jnp.zeros((HD, Q), jnp.float32)

    def settle(slot, n):
        high = psums[0]
        for h in range(1, HEADS):
            high = jnp.maximum(high, psums[h])
        fine = jnp.max(high) < 1e20

        @pl.when(fine)
        def _():
            for h in range(HEADS):
                tot[h] += psums[h]
                acc[h] += parts[h]

        @pl.when(jnp.logical_not(fine))
        def _():
            for h in range(HEADS):
                top = refs[h]
                for n in range(0, 1024, TILE):
                    s = jnp.dot(ks[slot][n:n + TILE], qs[h], preferred_element_type=jnp.float32)
                    top = jnp.maximum(top, jnp.max(s, axis=0, keepdims=True))
                keep = jnp.exp(refs[h] - top)
                psum, part = weigh(slot, h, top, tot[h] * keep, acc[h] * keep)
                tot[h] = psum
                acc[h] = part
                refs[h] = top

        @pl.when(lax.rem(n, 3) == 2)
        def _():
            b = n // 3
            line = lax.broadcasted_iota(jnp.int32, (128, Q), 0)
            new = jnp.zeros((128, Q), jnp.float32)
            for h in range(HEADS):
                total = jnp.sum(tot[h], axis=0, keepdims=True)
                new = jnp.where(line == h, refs[h], jnp.where(line == 4 + h, total, new))
            st_out[b] = new.T
            w_out[b] = acc[...].reshape(DL, Q).T

    def half(n, slot):
        real = jnp.minimum(n, NBLK - 1)
        c = lax.rem(real, 3)
        other = 1 - slot

        @pl.when(jnp.logical_and(c == 0, n < NBLK))
        def _():
            shifted(n // 3)

        @pl.when(n >= 2)
        def _():
            out_copy(n - 2, slot).wait()

        @pl.when(jnp.logical_and(n > 0, lax.rem(n - 1, 3) == 0))
        def _():
            restart(other)

        jobs = [(h, n) for h in range(HEADS) for n in range(0, 1024, TILE)]
        ahead = score(other, *jobs[0])
        state = {}
        now = ahead
        ahead = score(other, *jobs[1])
        f0 = conv_of(c, 0)
        absorb(other, state, now, *jobs[0])
        now = ahead
        ahead = score(other, *jobs[2])
        absorb(other, state, now, *jobs[1])
        now = ahead
        ahead = score(other, *jobs[3])
        keep_features(f0, slot, 0)
        project(f0, slot, 0)
        absorb(other, state, now, *jobs[2])
        now = ahead
        ahead = score(other, *jobs[4])
        absorb(other, state, now, *jobs[3])
        now = ahead
        ahead = score(other, *jobs[5])
        f1 = conv_of(c, 1)
        absorb(other, state, now, *jobs[4])
        now = ahead
        ahead = score(other, *jobs[6])
        absorb(other, state, now, *jobs[5])
        now = ahead
        ahead = score(other, *jobs[7])
        keep_features(f1, slot, 1)
        project(f1, slot, 1)
        absorb(other, state, now, *jobs[6])
        now = ahead
        absorb(other, state, now, *jobs[7])

        @pl.when(n < NBLK)
        def _():
            out_copy(n, slot).start()

        @pl.when(n > 0)
        def _():
            settle(other, n - 1)

    half(2 * step, 0)

    @pl.when(step < NBLK // 2)
    def _():
        half(2 * step + 1, 1)

    @pl.when(step == NBLK // 2)
    def _():
        out_copy(NBLK - 1, 1).wait()


def encode(xt, rows, cols, w2, kt, vt, queries):
    samples = xt.shape[0]
    whole = pl.BlockSpec(memory_space=pltpu.VMEM)
    return pl.pallas_call(
        encode_kernel,
        grid=(NBLK // 2 + 1,),
        out_shape=(
            jax.ShapeDtypeStruct((samples, 128, 12, 2, 128), jnp.bfloat16),
            jax.ShapeDtypeStruct((samples, Q, DL), jnp.float32),
            jax.ShapeDtypeStruct((samples, Q, 128), jnp.float32),
        ),
        in_specs=[whole] * 7,
        out_specs=(pl.BlockSpec(memory_space=pl.ANY), whole, whole),
        scratch_shapes=[
            pltpu.VMEM((26, KROW, 128), jnp.bfloat16),
            pltpu.VMEM((HEADS, DL, Q), jnp.bfloat16),
            pltpu.VMEM((1024, DL), jnp.bfloat16),
            pltpu.VMEM((1024, DL), jnp.bfloat16),
            pltpu.VMEM((DL, 1024), jnp.bfloat16),
            pltpu.VMEM((DL, 1024), jnp.bfloat16),
            pltpu.VMEM((128, 4, 2, 128), jnp.bfloat16),
            pltpu.VMEM((128, 4, 2, 128), jnp.bfloat16),
            pltpu.VMEM((HEADS, 1, Q), jnp.float32),
            pltpu.VMEM((HEADS, 8, Q), jnp.float32),
            pltpu.VMEM((HEADS, HD, Q), jnp.float32),
            pltpu.VMEM((HEADS, 8, Q), jnp.float32),
            pltpu.VMEM((HEADS, HD, Q), jnp.float32),
            pltpu.SemaphoreType.DMA((2,)),
        ],
        compiler_params=pltpu.CompilerParams(
            dimension_semantics=("arbitrary",), vmem_limit_bytes=40 * 1024 * 1024),
    )(xt, rows, cols, w2, kt, vt, queries)


def per_device(fields, conv_weight, kv_weight, out_weight, norm_gain, queries):
    samples, channels, lat_rows, lon_cols = fields.shape
    xt = jnp.pad(jnp.transpose(fields, (0, 2, 1, 3)), ((0, 0), (0, 0), (0, CP - channels), (0, 0)))
    conv_t = jnp.transpose(conv_weight, (0, 2, 1))
    rows, cols, w2, kt, vt = halo(xt, conv_t, kv_weight)
    feats, weighted, stats = encode(xt, rows, cols, w2, kt, vt, queries)
    features = feats.reshape(samples, 128, lat_rows, lon_cols)
    latents = reduce_all(weighted, stats, out_weight, norm_gain)
    return (features, latents.reshape(samples, Q, DL))


def solution(mesh):
    in_specs = (P(None, None, "lat", "lon"), P(), P(), P(), P(), P())
    out_specs = (P(None, None, "lat", "lon"), P())
    return jax.shard_map(
        per_device, mesh=mesh, in_specs=in_specs, out_specs=out_specs, check_vma=False
    )
```

```python
import functools
import jax
import jax.numpy as jnp
from jax import lax
from jax.experimental import pallas as pl
from jax.experimental.pallas import tpu as pltpu
from jax.sharding import PartitionSpec as P

DL = 256
Q = 256
HEADS = 4
HD = 64
MESH = pl.DeviceIdType.MESH
ROWS = 8
NCHIP = 64


def reduce_kernel(
    w_ref, st_ref, ow_ref, gain_ref, out_ref,
    half_w, half_st, msg, recv, gath,
    sem_a, sem_b, sem_c,
):
    lat = lax.axis_index("lat")
    lon = lax.axis_index("lon")
    core = lax.rem(lon, 2)
    chip = lat * 16 + lon // 2
    partner = lon + 1 - 2 * core

    def peer(k):
        c = lax.rem(chip + k, NCHIP)
        return (c // 16, lax.rem(c, 16) * 2 + core)

    barrier = pltpu.get_barrier_semaphore()
    pl.semaphore_signal(barrier, inc=1, device_id=(lat, partner), device_id_type=MESH)

    def greet(k, _):
        pl.semaphore_signal(barrier, inc=1, device_id=peer(k), device_id_type=MESH)
        return 0

    lax.fori_loop(1, NCHIP, greet, 0)
    pl.semaphore_wait(barrier, NCHIP)

    give = 2 - 2 * core
    keep = 2 * core
    cs = pltpu.make_async_remote_copy(
        st_ref.at[pl.ds(give, 2)], half_st, sem_a.at[0], sem_a.at[1],
        device_id=(lat, partner), device_id_type=MESH)
    cw = [
        pltpu.make_async_remote_copy(
            w_ref.at[give + i], half_w.at[i], sem_a.at[2 + 2 * i], sem_a.at[3 + 2 * i],
            device_id=(lat, partner), device_id_type=MESH)
        for i in range(2)
    ]
    cs.start()
    for c in cw:
        c.start()

    def limbs(v):
        a = v.astype(jnp.bfloat16).astype(jnp.float32)
        b = (v - a).astype(jnp.bfloat16).astype(jnp.float32)
        return [a, b, v - a - b]

    cs.wait()
    for i in range(2):
        s1 = st_ref[keep + i]
        s2 = half_st[i]
        peak = jnp.maximum(s1[0:4], s2[0:4])
        f1 = jnp.exp(s1[0:4] - peak)
        f2 = jnp.exp(s2[0:4] - peak)
        total = s1[4:8] * f1 + s2[4:8] * f2
        cw[i].wait()
        for h in range(HEADS):
            line = slice(h, h + 1)
            rows = slice(h * HD, (h + 1) * HD)
            value = w_ref[keep + i, rows] * f1[line] + half_w[i, rows] * f2[line]
            first = i * 32 + h * 8
            msg[first:first + 8, 0:ROWS] = value.reshape(8, ROWS, Q).astype(jnp.bfloat16)
            extra = jnp.concatenate(
                limbs(peak[line]) + limbs(total[line]) + [jnp.zeros((2, Q), jnp.float32)], axis=0)
            msg[first:first + 8, ROWS:2 * ROWS] = jnp.broadcast_to(extra[None], (8, ROWS, Q)).astype(jnp.bfloat16)

    def scatter(k, _):
        c = lax.rem(chip + k, NCHIP)
        pltpu.make_async_remote_copy(
            msg.at[c], recv.at[k - 1], sem_b.at[0], sem_b.at[1], device_id=peer(k), device_id_type=MESH).start()
        return 0

    lax.fori_loop(1, NCHIP, scatter, 0)
    own = msg[chip].astype(jnp.float32)
    pltpu.make_async_copy(recv, recv, sem_b.at[1]).wait()

    got = recv[...].astype(jnp.float32)
    extra = got[:, ROWS:2 * ROWS]
    m = extra[:, 0:1] + extra[:, 1:2] + extra[:, 2:3]
    t = extra[:, 3:4] + extra[:, 4:5] + extra[:, 5:6]
    own_m = own[8:9] + own[9:10] + own[10:11]
    own_t = own[11:12] + own[12:13] + own[13:14]
    top = jnp.maximum(jnp.max(m, axis=0), own_m)
    fac = jnp.exp(m - top[None])
    own_fac = jnp.exp(own_m - top)
    total = jnp.sum(fac * t, axis=0) + own_fac * own_t
    summed = jnp.sum(got[:, 0:ROWS] * fac, axis=0) + own[0:ROWS] * own_fac
    mine = core * NCHIP + chip
    gath[mine] = (summed / total).astype(jnp.bfloat16)

    def spread(k, _):
        pltpu.make_async_remote_copy(
            gath.at[mine], gath.at[mine], sem_c.at[0], sem_c.at[1], device_id=peer(k), device_id_type=MESH).start()
        return 0

    lax.fori_loop(1, NCHIP, spread, 0)
    pltpu.make_async_copy(recv, recv, sem_b.at[0]).wait()
    size = gath.at[pl.ds(0, NCHIP - 1)]
    pltpu.make_async_copy(size, size, sem_c.at[1]).wait()
    block = gath.at[pl.ds(core * NCHIP, NCHIP)]
    cg = pltpu.make_async_remote_copy(
        block, block, sem_c.at[2], sem_c.at[3], device_id=(lat, partner), device_id_type=MESH)
    cg.start()

    def finish(b):
        att = gath[pl.ds(b * 32, 32)].astype(jnp.float32).reshape(DL, Q).T.astype(jnp.bfloat16)
        proj = jnp.dot(att, ow_ref[...], preferred_element_type=jnp.float32)
        out_ref[b] = (
            proj * lax.rsqrt(jnp.mean(proj * proj, axis=-1, keepdims=True) + 1e-06) * gain_ref[...]
        )

    finish(keep)
    finish(keep + 1)
    cg.wait()
    finish(give)
    finish(give + 1)
    pltpu.make_async_copy(size, size, sem_c.at[0]).wait()


def reduce_all(weighted, stats, out_weight, norm_gain):
    vm = pl.BlockSpec(memory_space=pltpu.VMEM)
    return pl.pallas_call(
        reduce_kernel,
        out_shape=jax.ShapeDtypeStruct((4, Q, DL), jnp.float32),
        in_specs=[vm] * 4,
        out_specs=vm,
        scratch_shapes=[
            pltpu.VMEM((2, DL, Q), jnp.float32),
            pltpu.VMEM((2, 8, Q), jnp.float32),
            pltpu.VMEM((NCHIP, 2 * ROWS, Q), jnp.bfloat16),
            pltpu.VMEM((NCHIP - 1, 2 * ROWS, Q), jnp.bfloat16),
            pltpu.VMEM((2 * NCHIP, ROWS, Q), jnp.bfloat16),
            pltpu.SemaphoreType.DMA((6,)),
            pltpu.SemaphoreType.DMA((2,)),
            pltpu.SemaphoreType.DMA((4,)),
        ],
        compiler_params=pltpu.CompilerParams(
            collective_id=1, has_side_effects=True, vmem_limit_bytes=32 * 1024 * 1024
        ),
    )(weighted, stats, out_weight, norm_gain.reshape(1, DL))


CP = 80
KROW = 3 * CP
SCALE = HD ** (-0.5)
NT = (((1,), (1,)), ((), ()))


def halo_kernel(
    xt_ref, cw_ref, kv_ref, rows_ref, cols_ref, w2_ref, kt_ref, vt_ref,
    edge, got, taps, send_sem, recv_sem,
):
    lat = lax.axis_index("lat")
    lon = lax.axis_index("lon")
    nlat = lax.axis_size("lat")
    nlon = lax.axis_size("lon")
    right = lax.rem(lon + 1, nlon)
    left = lax.rem(lon + nlon - 1, nlon)
    barrier = pltpu.get_barrier_semaphore()

    def greet(dlat, dlon):
        pl.semaphore_signal(barrier, inc=1, device_id=(dlat, dlon), device_id_type=MESH)

    greet(lat, left)
    greet(lat, right)

    @pl.when(lat > 0)
    def _():
        greet(lat - 1, left)
        greet(lat - 1, lon)
        greet(lat - 1, right)

    @pl.when(lat < nlat - 1)
    def _():
        greet(lat + 1, left)
        greet(lat + 1, lon)
        greet(lat + 1, right)

    lane = lax.broadcasted_iota(jnp.int32, (CP, 128), 1)
    last = jnp.zeros((CP, 128), jnp.float32)
    first = jnp.zeros((CP, 128), jnp.float32)
    for b in range(xt_ref.shape[0]):
        for i in range(24):
            at = b * 24 + i
            row = xt_ref[b, i].astype(jnp.float32)
            turned = pltpu.roll(row, at + 1, 1)
            last = jnp.where(lane == at, turned, last)
            first = jnp.where(lane == at + 1, turned, first)
    edge[0] = last.astype(jnp.bfloat16)
    edge[1] = first.astype(jnp.bfloat16)

    def copy(src, dst, n, dlat, dlon):
        return pltpu.make_async_remote_copy(
            src, dst, send_sem.at[n], recv_sem.at[n], device_id=(dlat, dlon), device_id_type=MESH)

    same = [
        copy(edge.at[0], got.at[0, 0], 0, lat, right),
        copy(edge.at[1], got.at[1, 0], 1, lat, left),
    ]
    down = [
        copy(xt_ref.at[:, 23], rows_ref.at[0], 2, lat + 1, lon),
        copy(edge.at[0], got.at[0, 1], 3, lat + 1, right),
        copy(edge.at[1], got.at[1, 1], 4, lat + 1, left),
    ]
    up = [
        copy(xt_ref.at[:, 0], rows_ref.at[1], 5, lat - 1, lon),
        copy(edge.at[0], got.at[0, 2], 6, lat - 1, right),
        copy(edge.at[1], got.at[1, 2], 7, lat - 1, left),
    ]
    inner = jnp.logical_and(lat > 0, lat < nlat - 1)

    @pl.when(inner)
    def _():
        pl.semaphore_wait(barrier, 8)

    @pl.when(jnp.logical_not(inner))
    def _():
        pl.semaphore_wait(barrier, 5)

    for c in same:
        c.start()

    @pl.when(lat < nlat - 1)
    def _():
        for c in down:
            c.start()

    @pl.when(lat > 0)
    def _():
        for c in up:
            c.start()

    taps[...] = jnp.zeros_like(taps)
    for t in range(9):
        value = cw_ref[t].astype(jnp.float32)
        value = jnp.concatenate([value, jnp.zeros((CP - value.shape[0], 128), jnp.float32)], axis=0).astype(jnp.bfloat16)
        taps[t * CP:(t + 1) * CP, 0:128] = value
        taps[KROW + t * CP:KROW + (t + 1) * CP, 128:256] = value
    out_at = lax.broadcasted_iota(jnp.int32, (256, 256), 0)
    in_at = lax.broadcasted_iota(jnp.int32, (256, 256), 1)
    spread = jnp.where(out_at == jnp.where(in_at < 128, 2 * in_at, 2 * in_at - 255), 1.0, 0.0).astype(jnp.bfloat16)
    w2_ref[...] = lax.dot_general(spread, taps[...], NT, preferred_element_type=jnp.float32).astype(jnp.bfloat16)
    for r in range(2):
        some = spread[:, r * 128:(r + 1) * 128]
        kt_ref[:, r * DL:(r + 1) * DL] = lax.dot_general(
            some, kv_ref[0:DL], NT, preferred_element_type=jnp.float32).astype(jnp.bfloat16)
        vt_ref[r * DL:(r + 1) * DL] = lax.dot_general(
            kv_ref[DL:2 * DL], some, NT, preferred_element_type=jnp.float32).astype(jnp.bfloat16)

    for c in same:
        c.wait()

    @pl.when(lat > 0)
    def _():
        for c in down:
            c.wait_recv()
        for c in up:
            c.wait_send()

    @pl.when(lat < nlat - 1)
    def _():
        for c in up:
            c.wait_recv()
        for c in down:
            c.wait_send()

    @pl.when(lat == 0)
    def _():
        rows_ref[0] = jnp.zeros_like(rows_ref[0])
        for side in range(2):
            got[side, 1] = jnp.zeros((CP, 128), jnp.bfloat16)

    @pl.when(lat == nlat - 1)
    def _():
        rows_ref[1] = jnp.zeros_like(rows_ref[1])
        for side in range(2):
            got[side, 2] = jnp.zeros((CP, 128), jnp.bfloat16)

    for side in range(2):
        mid = got[side, 0].astype(jnp.float32)
        above = got[side, 1].astype(jnp.float32)
        below = got[side, 2].astype(jnp.float32)
        for b in range(4):
            at = b * 24 + side
            value = pltpu.roll(mid, (129 - at) % 128, 1)
            value = jnp.where(lane == 0, pltpu.roll(above, (128 - at - 23) % 128, 1), value)
            value = jnp.where(lane == 25, pltpu.roll(below, (128 + 25 - at) % 128, 1), value)
            cols_ref[side, b] = value.astype(jnp.bfloat16)


def halo(xt, conv_t, kv_weight):
    vm = pl.BlockSpec(memory_space=pltpu.VMEM)
    samples = xt.shape[0]
    return pl.pallas_call(
        halo_kernel,
        out_shape=(
            jax.ShapeDtypeStruct((2, samples, CP, 128), jnp.bfloat16),
            jax.ShapeDtypeStruct((2, samples, CP, 128), jnp.bfloat16),
            jax.ShapeDtypeStruct((256, 4 * KROW), jnp.bfloat16),
            jax.ShapeDtypeStruct((256, 512), jnp.bfloat16),
            jax.ShapeDtypeStruct((512, 256), jnp.bfloat16),
        ),
        in_specs=[vm] * 3,
        out_specs=(vm,) * 5,
        scratch_shapes=[
            pltpu.VMEM((2, CP, 128), jnp.bfloat16),
            pltpu.VMEM((2, 3, CP, 128), jnp.bfloat16),
            pltpu.VMEM((4 * KROW, 256), jnp.bfloat16),
            pltpu.SemaphoreType.DMA((8,)),
            pltpu.SemaphoreType.DMA((8,)),
        ],
        compiler_params=pltpu.CompilerParams(
            collective_id=0, has_side_effects=True, vmem_limit_bytes=32 * 1024 * 1024),
    )(xt, conv_t, kv_weight)


NBLK = 12
TILE = 512


def encode_kernel(
    xt_ref, rows_ref, cols_ref, w2_ref, kt_ref, vt_ref, q_ref, feat_ref, w_out, st_out,
    x3, qs, k_a, k_b, v_a, v_b, feat_a, feat_b, refs, tot, acc, psums, parts, sem,
):
    step = pl.program_id(0)
    ks = (k_a, k_b)
    vs = (v_a, v_b)
    fbuf = (feat_a, feat_b)
    lane = lax.broadcasted_iota(jnp.int32, (CP, 128), 1)

    @pl.when(step == 0)
    def _():
        turned = (q_ref[...].astype(jnp.float32) * SCALE).T
        owner = lax.broadcasted_iota(jnp.int32, (DL, Q), 0) // HD
        for h in range(HEADS):
            qs[h] = jnp.where(owner == h, turned, 0.0).astype(jnp.bfloat16)

    def put_row(slot, i, row, lo, hi):
        before = jnp.where(lane == 0, lo, pltpu.roll(row, 1, 1))
        after = jnp.where(lane == 127, hi, pltpu.roll(row, 127, 1))
        x3[slot, i, 0:CP] = before
        x3[slot, i, CP:2 * CP] = row
        x3[slot, i, 2 * CP:3 * CP] = after

    def outer_rows(b, slot):
        lo = cols_ref[0, b]
        hi = cols_ref[1, b]
        put_row(slot, 0, rows_ref[0, b], lo, pltpu.roll(hi, 127, 1))
        put_row(slot, 25, rows_ref[1, b], pltpu.roll(lo, 103, 1), pltpu.roll(hi, 102, 1))

    def inner_rows(b, slot, c):
        lo = pltpu.roll(cols_ref[0, b], 128 - 8 * c, 1) if isinstance(c, int) and c > 0 else cols_ref[0, b]
        hi = pltpu.roll(cols_ref[1, b], 128 - 8 * c, 1) if isinstance(c, int) and c > 0 else cols_ref[1, b]
        if not isinstance(c, int):
            lo = pltpu.roll(lo.astype(jnp.float32), lax.rem(128 - 8 * c, 128), 1).astype(jnp.bfloat16)
            hi = pltpu.roll(hi.astype(jnp.float32), lax.rem(128 - 8 * c, 128), 1).astype(jnp.bfloat16)
        for j in range(8):
            put_row(slot, 8 * c + 1 + j, xt_ref[b, 8 * c + j],
                    pltpu.roll(lo, 127 - j, 1), pltpu.roll(hi, 126 - j, 1))

    def out_copy(n, slot):
        return pltpu.make_async_copy(
            fbuf[slot], feat_ref.at[n // 3, :, pl.ds(lax.rem(n, 3) * 4, 4)], sem.at[slot])

    def conv_of(b, c, g):
        base = c * 8 + g * 4
        one = x3[lax.rem(b, 2), pl.ds(base, 4)].reshape(4 * KROW, 128)
        two = x3[lax.rem(b, 2), pl.ds(base + 2, 4)].reshape(4 * KROW, 128)
        both = jnp.concatenate([one, two], axis=1)
        conv = jnp.dot(w2_ref[...], both, preferred_element_type=jnp.float32)
        return jax.nn.gelu(conv, approximate=True).astype(jnp.bfloat16)

    def keep_features(feats, slot, g):
        fbuf[slot][:, 2 * g] = feats[:, 0:128].reshape(128, 2, 128)
        fbuf[slot][:, 2 * g + 1] = feats[:, 128:256].reshape(128, 2, 128)

    def project(feats, slot, g):
        turned = feats.T
        values = jnp.dot(vt_ref[...], feats, preferred_element_type=jnp.float32).astype(jnp.bfloat16)
        keys = jnp.dot(turned, kt_ref[...], preferred_element_type=jnp.float32).astype(jnp.bfloat16)
        for r in range(2):
            at = r * 512 + g * 256
            vs[slot][:, at:at + 256] = values[r * DL:(r + 1) * DL]
            ks[slot][at:at + 256] = keys[:, r * DL:(r + 1) * DL]

    def weigh(slot, h, ref, psum, part):
        for n in range(0, 1024, TILE):
            s = jnp.dot(ks[slot][n:n + TILE], qs[h], preferred_element_type=jnp.float32)
            p = jnp.exp(s - ref)
            psum = psum + jnp.sum(p.reshape(TILE // 8, 8, Q), axis=0)
            part = part + jnp.dot(
                vs[slot][h * HD:(h + 1) * HD, n:n + TILE], p.astype(jnp.bfloat16), preferred_element_type=jnp.float32)
        return psum, part

    def score(slot, h, n):
        return jnp.dot(ks[slot][n:n + TILE], qs[h], preferred_element_type=jnp.float32)

    def absorb(slot, state, s, h, n):
        p = jnp.exp(s - refs[h])
        psum = jnp.sum(p.reshape(TILE // 8, 8, Q), axis=0)
        part = jnp.dot(
            vs[slot][h * HD:(h + 1) * HD, n:n + TILE], p.astype(jnp.bfloat16), preferred_element_type=jnp.float32)
        if n > 0:
            psum = psum + state[h][0]
            part = part + state[h][1]
        state[h] = (psum, part)
        if n + TILE == 1024:
            psums[h] = psum
            parts[h] = part

    def head(slot, h):
        psum, part = weigh(slot, h, refs[h], jnp.zeros((8, Q), jnp.float32), jnp.zeros((HD, Q), jnp.float32))
        psums[h] = psum
        parts[h] = part

    def restart(slot):
        for h in range(HEADS):
            s = jnp.dot(ks[slot][0:128], qs[h], preferred_element_type=jnp.float32)
            refs[h] = jnp.max(s, axis=0, keepdims=True)
            tot[h] = jnp.zeros((8, Q), jnp.float32)
            acc[h] = jnp.zeros((HD, Q), jnp.float32)

    def settle(slot, n):
        high = psums[0]
        for h in range(1, HEADS):
            high = jnp.maximum(high, psums[h])
        fine = jnp.max(high) < 1e20

        @pl.when(fine)
        def _():
            for h in range(HEADS):
                tot[h] += psums[h]
                acc[h] += parts[h]

        @pl.when(jnp.logical_not(fine))
        def _():
            for h in range(HEADS):
                top = refs[h]
                for n in range(0, 1024, TILE):
                    s = jnp.dot(ks[slot][n:n + TILE], qs[h], preferred_element_type=jnp.float32)
                    top = jnp.maximum(top, jnp.max(s, axis=0, keepdims=True))
                keep = jnp.exp(refs[h] - top)
                psum, part = weigh(slot, h, top, tot[h] * keep, acc[h] * keep)
                tot[h] = psum
                acc[h] = part
                refs[h] = top

        @pl.when(lax.rem(n, 3) == 2)
        def _():
            b = n // 3
            line = lax.broadcasted_iota(jnp.int32, (8, Q), 0)
            new = jnp.zeros((8, Q), jnp.float32)
            for h in range(HEADS):
                total = jnp.sum(tot[h], axis=0, keepdims=True)
                new = jnp.where(line == h, refs[h], jnp.where(line == 4 + h, total, new))
            st_out[b] = new
            w_out[b] = acc[...].reshape(DL, Q)

    def half(n, slot, begin, end):
        b = n // 3
        c = lax.rem(n, 3)
        other = 1 - slot

        @pl.when(jnp.logical_and(c == 0, n < NBLK))
        def _():
            outer_rows(b, lax.rem(b, 2))

        @pl.when(n >= 2)
        def _():
            out_copy(n - 2, slot).wait()

        @pl.when(jnp.logical_and(n > 0, lax.rem(n - 1, 3) == 0))
        def _():
            restart(other)

        if begin:
            @pl.when(n == 0)
            def _():
                for part in range(3):
                    inner_rows(0, 0, part)
                inner_rows(1, 1, 0)
                f0 = conv_of(b, c, 0)
                f1 = conv_of(b, c, 1)
                keep_features(f0, slot, 0)
                project(f0, slot, 0)
                keep_features(f1, slot, 1)
                project(f1, slot, 1)

        def mixed():
            after = jnp.minimum(b + 1, xt_ref.shape[0] - 1)
            next_slot = lax.rem(b + 1, 2)
            jobs = [(h, n) for h in range(HEADS) for n in range(0, 1024, TILE)]
            ahead = score(other, *jobs[0])
            state = {}
            now = ahead
            ahead = score(other, *jobs[1])
            f0 = conv_of(b, c, 0)
            absorb(other, state, now, *jobs[0])
            now = ahead
            ahead = score(other, *jobs[2])
            f1 = conv_of(b, c, 1)
            inner_rows(after, next_slot, c)
            absorb(other, state, now, *jobs[1])
            now = ahead
            ahead = score(other, *jobs[3])
            absorb(other, state, now, *jobs[2])
            now = ahead
            ahead = score(other, *jobs[4])
            keep_features(f0, slot, 0)
            project(f0, slot, 0)
            absorb(other, state, now, *jobs[3])
            now = ahead
            ahead = score(other, *jobs[5])
            absorb(other, state, now, *jobs[4])
            now = ahead
            ahead = score(other, *jobs[6])
            keep_features(f1, slot, 1)
            project(f1, slot, 1)
            absorb(other, state, now, *jobs[5])
            now = ahead
            ahead = score(other, *jobs[7])
            absorb(other, state, now, *jobs[6])
            now = ahead
            absorb(other, state, now, *jobs[7])

        if begin or end:
            pl.when(jnp.logical_and(n > 0, n < NBLK))(mixed)
        else:
            mixed()

        if end:
            @pl.when(n == NBLK)
            def _():
                jobs = [(h, n) for h in range(HEADS) for n in range(0, 1024, TILE)]
                ahead = score(other, *jobs[0])
                state = {}
                now = ahead
                ahead = score(other, *jobs[1])
                absorb(other, state, now, *jobs[0])
                now = ahead
                ahead = score(other, *jobs[2])
                absorb(other, state, now, *jobs[1])
                now = ahead
                ahead = score(other, *jobs[3])
                absorb(other, state, now, *jobs[2])
                now = ahead
                ahead = score(other, *jobs[4])
                absorb(other, state, now, *jobs[3])
                now = ahead
                ahead = score(other, *jobs[5])
                absorb(other, state, now, *jobs[4])
                now = ahead
                ahead = score(other, *jobs[6])
                absorb(other, state, now, *jobs[5])
                now = ahead
                ahead = score(other, *jobs[7])
                absorb(other, state, now, *jobs[6])
                now = ahead
                absorb(other, state, now, *jobs[7])

        @pl.when(n < NBLK)
        def _():
            out_copy(n, slot).start()

        @pl.when(n > 0)
        def _():
            settle(other, n - 1)

    half(2 * step, 0, True, True)

    @pl.when(step < NBLK // 2)
    def _():
        half(2 * step + 1, 1, False, False)

    @pl.when(step == NBLK // 2)
    def _():
        out_copy(NBLK - 1, 1).wait()


def encode(xt, rows, cols, w2, kt, vt, queries):
    samples = xt.shape[0]
    whole = pl.BlockSpec(memory_space=pltpu.VMEM)
    return pl.pallas_call(
        encode_kernel,
        grid=(NBLK // 2 + 1,),
        out_shape=(
            jax.ShapeDtypeStruct((samples, 128, 12, 2, 128), jnp.bfloat16),
            jax.ShapeDtypeStruct((samples, DL, Q), jnp.float32),
            jax.ShapeDtypeStruct((samples, 8, Q), jnp.float32),
        ),
        in_specs=[whole] * 7,
        out_specs=(pl.BlockSpec(memory_space=pl.ANY), whole, whole),
        scratch_shapes=[
            pltpu.VMEM((2, 26, KROW, 128), jnp.bfloat16),
            pltpu.VMEM((HEADS, DL, Q), jnp.bfloat16),
            pltpu.VMEM((1024, DL), jnp.bfloat16),
            pltpu.VMEM((1024, DL), jnp.bfloat16),
            pltpu.VMEM((DL, 1024), jnp.bfloat16),
            pltpu.VMEM((DL, 1024), jnp.bfloat16),
            pltpu.VMEM((128, 4, 2, 128), jnp.bfloat16),
            pltpu.VMEM((128, 4, 2, 128), jnp.bfloat16),
            pltpu.VMEM((HEADS, 1, Q), jnp.float32),
            pltpu.VMEM((HEADS, 8, Q), jnp.float32),
            pltpu.VMEM((HEADS, HD, Q), jnp.float32),
            pltpu.VMEM((HEADS, 8, Q), jnp.float32),
            pltpu.VMEM((HEADS, HD, Q), jnp.float32),
            pltpu.SemaphoreType.DMA((2,)),
        ],
        compiler_params=pltpu.CompilerParams(
            dimension_semantics=("arbitrary",), vmem_limit_bytes=40 * 1024 * 1024),
    )(xt, rows, cols, w2, kt, vt, queries)


def per_device(fields, conv_weight, kv_weight, out_weight, norm_gain, queries):
    samples, channels, lat_rows, lon_cols = fields.shape
    xt = jnp.pad(jnp.transpose(fields, (0, 2, 1, 3)), ((0, 0), (0, 0), (0, CP - channels), (0, 0)))
    conv_t = jnp.transpose(conv_weight, (0, 2, 1))
    rows, cols, w2, kt, vt = halo(xt, conv_t, kv_weight)
    feats, weighted, stats = encode(xt, rows, cols, w2, kt, vt, queries)
    features = feats.reshape(samples, 128, lat_rows, lon_cols)
    latents = reduce_all(weighted, stats, out_weight, norm_gain)
    return (features, latents)


def solution(mesh):
    in_specs = (P(None, None, "lat", "lon"), P(), P(), P(), P(), P())
    out_specs = (P(None, None, "lat", "lon"), P())
    return jax.shard_map(
        per_device, mesh=mesh, in_specs=in_specs, out_specs=out_specs, check_vma=False
    )
```

```python
import functools
import jax
import jax.numpy as jnp
from jax import lax
from jax.experimental import pallas as pl
from jax.experimental.pallas import tpu as pltpu
from jax.sharding import PartitionSpec as P

DL = 256
Q = 256
HEADS = 4
HD = 64
MESH = pl.DeviceIdType.MESH
ROWS = 8
NCHIP = 64


def reduce_kernel(
    w_in, st_in, k_ref, v_ref, q_ref, ow_ref, gain_ref, out_ref,
    w_ref, st_ref, half_w, half_st, msg, recv, gath,
    sem_a, sem_b, sem_c,
):
    lat = lax.axis_index("lat")
    lon = lax.axis_index("lon")
    core = lax.rem(lon, 2)
    chip = lat * 16 + lon // 2
    partner = lon + 1 - 2 * core

    def peer(k):
        c = lax.rem(chip + k, NCHIP)
        return (c // 16, lax.rem(c, 16) * 2 + core)

    barrier = pltpu.get_barrier_semaphore()
    pl.semaphore_signal(barrier, inc=1, device_id=(lat, partner), device_id_type=MESH)

    def greet(k, _):
        pl.semaphore_signal(barrier, inc=1, device_id=peer(k), device_id_type=MESH)
        return 0

    lax.fori_loop(1, NCHIP, greet, 0)

    def score(h):
        return jnp.dot(k_ref[...], q_ref[h], preferred_element_type=jnp.float32)

    tops, totals = [], []
    ahead = score(0)
    for h in range(HEADS):
        s = ahead
        if h + 1 < HEADS:
            ahead = score(h + 1)
        rows = slice(h * HD, (h + 1) * HD)
        before = st_in[3, h:h + 1]
        top = jnp.maximum(jnp.max(s, axis=0, keepdims=True), before)
        p = jnp.exp(s - top)
        shrink = jnp.exp(before - top)
        part = jnp.dot(v_ref[rows], p.astype(jnp.bfloat16), preferred_element_type=jnp.float32)
        w_ref[3, rows] = part + w_in[3, rows] * shrink
        tops.append(top)
        totals.append(jnp.sum(p, axis=0, keepdims=True) + st_in[3, 4 + h:5 + h] * shrink)
    st_ref[3] = jnp.concatenate(tops + totals, axis=0)
    for i in range(3):
        w_ref[i] = w_in[i]
        st_ref[i] = st_in[i]
    pl.semaphore_wait(barrier, NCHIP)

    give = 2 - 2 * core
    keep = 2 * core
    cs = pltpu.make_async_remote_copy(
        st_ref.at[pl.ds(give, 2)], half_st, sem_a.at[0], sem_a.at[1],
        device_id=(lat, partner), device_id_type=MESH)
    cw = [
        pltpu.make_async_remote_copy(
            w_ref.at[give + i], half_w.at[i], sem_a.at[2 + 2 * i], sem_a.at[3 + 2 * i],
            device_id=(lat, partner), device_id_type=MESH)
        for i in range(2)
    ]
    cs.start()
    for c in cw:
        c.start()

    def limbs(v):
        a = v.astype(jnp.bfloat16).astype(jnp.float32)
        b = (v - a).astype(jnp.bfloat16).astype(jnp.float32)
        return [a, b, v - a - b]

    cs.wait()
    for i in range(2):
        s1 = st_ref[keep + i]
        s2 = half_st[i]
        peak = jnp.maximum(s1[0:4], s2[0:4])
        f1 = jnp.exp(s1[0:4] - peak)
        f2 = jnp.exp(s2[0:4] - peak)
        total = s1[4:8] * f1 + s2[4:8] * f2
        cw[i].wait()
        for h in range(HEADS):
            line = slice(h, h + 1)
            rows = slice(h * HD, (h + 1) * HD)
            value = w_ref[keep + i, rows] * f1[line] + half_w[i, rows] * f2[line]
            first = i * 32 + h * 8
            msg[first:first + 8, 0:ROWS] = value.reshape(8, ROWS, Q).astype(jnp.bfloat16)
            extra = jnp.concatenate(
                limbs(peak[line]) + limbs(total[line]) + [jnp.zeros((2, Q), jnp.float32)], axis=0)
            msg[first:first + 8, ROWS:2 * ROWS] = jnp.broadcast_to(extra[None], (8, ROWS, Q)).astype(jnp.bfloat16)

    def scatter(k, _):
        c = lax.rem(chip + k, NCHIP)
        pltpu.make_async_remote_copy(
            msg.at[c], recv.at[k - 1], sem_b.at[0], sem_b.at[1], device_id=peer(k), device_id_type=MESH).start()
        return 0

    lax.fori_loop(1, NCHIP, scatter, 0)
    own = msg[chip].astype(jnp.float32)
    pltpu.make_async_copy(recv, recv, sem_b.at[1]).wait()

    got = recv[...].astype(jnp.float32)
    extra = got[:, ROWS:2 * ROWS]
    m = extra[:, 0:1] + extra[:, 1:2] + extra[:, 2:3]
    t = extra[:, 3:4] + extra[:, 4:5] + extra[:, 5:6]
    own_m = own[8:9] + own[9:10] + own[10:11]
    own_t = own[11:12] + own[12:13] + own[13:14]
    top = jnp.maximum(jnp.max(m, axis=0), own_m)
    fac = jnp.exp(m - top[None])
    own_fac = jnp.exp(own_m - top)
    total = jnp.sum(fac * t, axis=0) + own_fac * own_t
    summed = jnp.sum(got[:, 0:ROWS] * fac, axis=0) + own[0:ROWS] * own_fac
    mine = core * NCHIP + chip
    gath[mine] = (summed / total).astype(jnp.bfloat16)

    def spread(k, _):
        pltpu.make_async_remote_copy(
            gath.at[mine], gath.at[mine], sem_c.at[0], sem_c.at[1], device_id=peer(k), device_id_type=MESH).start()
        return 0

    lax.fori_loop(1, NCHIP, spread, 0)
    pltpu.make_async_copy(recv, recv, sem_b.at[0]).wait()
    size = gath.at[pl.ds(0, NCHIP - 1)]
    pltpu.make_async_copy(size, size, sem_c.at[1]).wait()
    block = gath.at[pl.ds(core * NCHIP, NCHIP)]
    cg = pltpu.make_async_remote_copy(
        block, block, sem_c.at[2], sem_c.at[3], device_id=(lat, partner), device_id_type=MESH)
    cg.start()

    def finish(b):
        att = gath[pl.ds(b * 32, 32)].astype(jnp.float32).reshape(DL, Q).T.astype(jnp.bfloat16)
        proj = jnp.dot(att, ow_ref[...], preferred_element_type=jnp.float32)
        out_ref[b] = (
            proj * lax.rsqrt(jnp.mean(proj * proj, axis=-1, keepdims=True) + 1e-06) * gain_ref[...]
        )

    finish(keep)
    finish(keep + 1)
    cg.wait()
    finish(give)
    finish(give + 1)
    pltpu.make_async_copy(size, size, sem_c.at[0]).wait()


def reduce_all(weighted, stats, keys, values, turned, out_weight, norm_gain):
    vm = pl.BlockSpec(memory_space=pltpu.VMEM)
    return pl.pallas_call(
        reduce_kernel,
        out_shape=jax.ShapeDtypeStruct((4, Q, DL), jnp.float32),
        in_specs=[vm] * 7,
        out_specs=vm,
        scratch_shapes=[
            pltpu.VMEM((4, DL, Q), jnp.float32),
            pltpu.VMEM((4, 8, Q), jnp.float32),
            pltpu.VMEM((2, DL, Q), jnp.float32),
            pltpu.VMEM((2, 8, Q), jnp.float32),
            pltpu.VMEM((NCHIP, 2 * ROWS, Q), jnp.bfloat16),
            pltpu.VMEM((NCHIP - 1, 2 * ROWS, Q), jnp.bfloat16),
            pltpu.VMEM((2 * NCHIP, ROWS, Q), jnp.bfloat16),
            pltpu.SemaphoreType.DMA((6,)),
            pltpu.SemaphoreType.DMA((2,)),
            pltpu.SemaphoreType.DMA((4,)),
        ],
        compiler_params=pltpu.CompilerParams(
            collective_id=1, has_side_effects=True, vmem_limit_bytes=32 * 1024 * 1024
        ),
    )(weighted, stats, keys, values, turned, out_weight, norm_gain.reshape(1, DL))


CP = 80
KROW = 3 * CP
SCALE = HD ** (-0.5)
NT = (((1,), (1,)), ((), ()))


def halo_kernel(
    xt_ref, cw_ref, kv_ref, rows_ref, cols_ref, w2_ref, kt_ref, vt_ref,
    edge, got, taps, send_sem, recv_sem,
):
    lat = lax.axis_index("lat")
    lon = lax.axis_index("lon")
    nlat = lax.axis_size("lat")
    nlon = lax.axis_size("lon")
    right = lax.rem(lon + 1, nlon)
    left = lax.rem(lon + nlon - 1, nlon)
    barrier = pltpu.get_barrier_semaphore()

    def greet(dlat, dlon):
        pl.semaphore_signal(barrier, inc=1, device_id=(dlat, dlon), device_id_type=MESH)

    greet(lat, left)
    greet(lat, right)

    @pl.when(lat > 0)
    def _():
        greet(lat - 1, left)
        greet(lat - 1, lon)
        greet(lat - 1, right)

    @pl.when(lat < nlat - 1)
    def _():
        greet(lat + 1, left)
        greet(lat + 1, lon)
        greet(lat + 1, right)

    lane = lax.broadcasted_iota(jnp.int32, (CP, 128), 1)
    last = jnp.zeros((CP, 128), jnp.float32)
    first = jnp.zeros((CP, 128), jnp.float32)
    for b in range(xt_ref.shape[0]):
        for i in range(24):
            at = b * 24 + i
            row = xt_ref[b, i].astype(jnp.float32)
            turned = pltpu.roll(row, at + 1, 1)
            last = jnp.where(lane == at, turned, last)
            first = jnp.where(lane == at + 1, turned, first)
    edge[0] = last.astype(jnp.bfloat16)
    edge[1] = first.astype(jnp.bfloat16)

    def copy(src, dst, n, dlat, dlon):
        return pltpu.make_async_remote_copy(
            src, dst, send_sem.at[n], recv_sem.at[n], device_id=(dlat, dlon), device_id_type=MESH)

    same = [
        copy(edge.at[0], got.at[0, 0], 0, lat, right),
        copy(edge.at[1], got.at[1, 0], 1, lat, left),
    ]
    down = [
        copy(xt_ref.at[:, 23], rows_ref.at[0], 2, lat + 1, lon),
        copy(edge.at[0], got.at[0, 1], 3, lat + 1, right),
        copy(edge.at[1], got.at[1, 1], 4, lat + 1, left),
    ]
    up = [
        copy(xt_ref.at[:, 0], rows_ref.at[1], 5, lat - 1, lon),
        copy(edge.at[0], got.at[0, 2], 6, lat - 1, right),
        copy(edge.at[1], got.at[1, 2], 7, lat - 1, left),
    ]
    inner = jnp.logical_and(lat > 0, lat < nlat - 1)

    @pl.when(inner)
    def _():
        pl.semaphore_wait(barrier, 8)

    @pl.when(jnp.logical_not(inner))
    def _():
        pl.semaphore_wait(barrier, 5)

    for c in same:
        c.start()

    @pl.when(lat < nlat - 1)
    def _():
        for c in down:
            c.start()

    @pl.when(lat > 0)
    def _():
        for c in up:
            c.start()

    taps[...] = jnp.zeros_like(taps)
    for t in range(9):
        value = cw_ref[t].astype(jnp.float32)
        value = jnp.concatenate([value, jnp.zeros((CP - value.shape[0], 128), jnp.float32)], axis=0).astype(jnp.bfloat16)
        taps[t * CP:(t + 1) * CP, 0:128] = value
        taps[KROW + t * CP:KROW + (t + 1) * CP, 128:256] = value
    out_at = lax.broadcasted_iota(jnp.int32, (256, 256), 0)
    in_at = lax.broadcasted_iota(jnp.int32, (256, 256), 1)
    spread = jnp.where(out_at == jnp.where(in_at < 128, 2 * in_at, 2 * in_at - 255), 1.0, 0.0).astype(jnp.bfloat16)
    w2_ref[...] = lax.dot_general(spread, taps[...], NT, preferred_element_type=jnp.float32).astype(jnp.bfloat16)
    for r in range(2):
        some = spread[:, r * 128:(r + 1) * 128]
        kt_ref[:, r * DL:(r + 1) * DL] = lax.dot_general(
            some, kv_ref[0:DL], NT, preferred_element_type=jnp.float32).astype(jnp.bfloat16)
        vt_ref[r * DL:(r + 1) * DL] = lax.dot_general(
            kv_ref[DL:2 * DL], some, NT, preferred_element_type=jnp.float32).astype(jnp.bfloat16)

    for c in same:
        c.wait()

    @pl.when(lat > 0)
    def _():
        for c in down:
            c.wait_recv()
        for c in up:
            c.wait_send()

    @pl.when(lat < nlat - 1)
    def _():
        for c in up:
            c.wait_recv()
        for c in down:
            c.wait_send()

    @pl.when(lat == 0)
    def _():
        rows_ref[0] = jnp.zeros_like(rows_ref[0])
        for side in range(2):
            got[side, 1] = jnp.zeros((CP, 128), jnp.bfloat16)

    @pl.when(lat == nlat - 1)
    def _():
        rows_ref[1] = jnp.zeros_like(rows_ref[1])
        for side in range(2):
            got[side, 2] = jnp.zeros((CP, 128), jnp.bfloat16)

    for side in range(2):
        mid = got[side, 0].astype(jnp.float32)
        above = got[side, 1].astype(jnp.float32)
        below = got[side, 2].astype(jnp.float32)
        for b in range(4):
            at = b * 24 + side
            value = pltpu.roll(mid, (129 - at) % 128, 1)
            value = jnp.where(lane == 0, pltpu.roll(above, (128 - at - 23) % 128, 1), value)
            value = jnp.where(lane == 25, pltpu.roll(below, (128 + 25 - at) % 128, 1), value)
            cols_ref[side, b] = value.astype(jnp.bfloat16)


def halo(xt, conv_t, kv_weight):
    vm = pl.BlockSpec(memory_space=pltpu.VMEM)
    samples = xt.shape[0]
    return pl.pallas_call(
        halo_kernel,
        out_shape=(
            jax.ShapeDtypeStruct((2, samples, CP, 128), jnp.bfloat16),
            jax.ShapeDtypeStruct((2, samples, CP, 128), jnp.bfloat16),
            jax.ShapeDtypeStruct((256, 4 * KROW), jnp.bfloat16),
            jax.ShapeDtypeStruct((256, 512), jnp.bfloat16),
            jax.ShapeDtypeStruct((512, 256), jnp.bfloat16),
        ),
        in_specs=[vm] * 3,
        out_specs=(vm,) * 5,
        scratch_shapes=[
            pltpu.VMEM((2, CP, 128), jnp.bfloat16),
            pltpu.VMEM((2, 3, CP, 128), jnp.bfloat16),
            pltpu.VMEM((4 * KROW, 256), jnp.bfloat16),
            pltpu.SemaphoreType.DMA((8,)),
            pltpu.SemaphoreType.DMA((8,)),
        ],
        compiler_params=pltpu.CompilerParams(
            collective_id=0, has_side_effects=True, vmem_limit_bytes=32 * 1024 * 1024),
    )(xt, conv_t, kv_weight)


NBLK = 12
TILE = 512


def encode_kernel(
    xt_ref, rows_ref, cols_ref, w2_ref, kt_ref, vt_ref, q_ref, feat_ref, w_out, st_out, k_out, v_out, q_out,
    x3, qs, k_a, k_b, v_a, v_b, feat_a, feat_b, refs, tot, acc, psums, parts, sem,
):
    step = pl.program_id(0)
    ks = (k_a, k_b)
    vs = (v_a, v_b)
    fbuf = (feat_a, feat_b)
    lane = lax.broadcasted_iota(jnp.int32, (CP, 128), 1)

    @pl.when(step == 0)
    def _():
        turned = (q_ref[...].astype(jnp.float32) * SCALE).T
        owner = lax.broadcasted_iota(jnp.int32, (DL, Q), 0) // HD
        for h in range(HEADS):
            qs[h] = jnp.where(owner == h, turned, 0.0).astype(jnp.bfloat16)

    def put_row(slot, i, row, lo, hi):
        before = jnp.where(lane == 0, lo, pltpu.roll(row, 1, 1))
        after = jnp.where(lane == 127, hi, pltpu.roll(row, 127, 1))
        x3[slot, i, 0:CP] = before
        x3[slot, i, CP:2 * CP] = row
        x3[slot, i, 2 * CP:3 * CP] = after

    def outer_rows(b, slot):
        lo = cols_ref[0, b]
        hi = cols_ref[1, b]
        put_row(slot, 0, rows_ref[0, b], lo, pltpu.roll(hi, 127, 1))
        put_row(slot, 25, rows_ref[1, b], pltpu.roll(lo, 103, 1), pltpu.roll(hi, 102, 1))

    def inner_rows(b, slot, c):
        lo = pltpu.roll(cols_ref[0, b], 128 - 8 * c, 1) if isinstance(c, int) and c > 0 else cols_ref[0, b]
        hi = pltpu.roll(cols_ref[1, b], 128 - 8 * c, 1) if isinstance(c, int) and c > 0 else cols_ref[1, b]
        if not isinstance(c, int):
            lo = pltpu.roll(lo.astype(jnp.float32), lax.rem(128 - 8 * c, 128), 1).astype(jnp.bfloat16)
            hi = pltpu.roll(hi.astype(jnp.float32), lax.rem(128 - 8 * c, 128), 1).astype(jnp.bfloat16)
        for j in range(8):
            put_row(slot, 8 * c + 1 + j, xt_ref[b, 8 * c + j],
                    pltpu.roll(lo, 127 - j, 1), pltpu.roll(hi, 126 - j, 1))

    def out_copy(n, slot):
        return pltpu.make_async_copy(
            fbuf[slot], feat_ref.at[n // 3, :, pl.ds(lax.rem(n, 3) * 4, 4)], sem.at[slot])

    def conv_of(b, c, g):
        base = c * 8 + g * 4
        one = x3[lax.rem(b, 2), pl.ds(base, 4)].reshape(4 * KROW, 128)
        two = x3[lax.rem(b, 2), pl.ds(base + 2, 4)].reshape(4 * KROW, 128)
        both = jnp.concatenate([one, two], axis=1)
        conv = jnp.dot(w2_ref[...], both, preferred_element_type=jnp.float32)
        return jax.nn.gelu(conv, approximate=True).astype(jnp.bfloat16)

    def keep_features(feats, slot, g):
        fbuf[slot][:, 2 * g] = feats[:, 0:128].reshape(128, 2, 128)
        fbuf[slot][:, 2 * g + 1] = feats[:, 128:256].reshape(128, 2, 128)

    def project(feats, slot, g):
        turned = feats.T
        values = jnp.dot(vt_ref[...], feats, preferred_element_type=jnp.float32).astype(jnp.bfloat16)
        keys = jnp.dot(turned, kt_ref[...], preferred_element_type=jnp.float32).astype(jnp.bfloat16)
        for r in range(2):
            at = r * 512 + g * 256
            vs[slot][:, at:at + 256] = values[r * DL:(r + 1) * DL]
            ks[slot][at:at + 256] = keys[:, r * DL:(r + 1) * DL]

    def weigh(slot, h, ref, psum, part):
        for n in range(0, 1024, TILE):
            s = jnp.dot(ks[slot][n:n + TILE], qs[h], preferred_element_type=jnp.float32)
            p = jnp.exp(s - ref)
            psum = psum + jnp.sum(p.reshape(TILE // 8, 8, Q), axis=0)
            part = part + jnp.dot(
                vs[slot][h * HD:(h + 1) * HD, n:n + TILE], p.astype(jnp.bfloat16), preferred_element_type=jnp.float32)
        return psum, part

    def score(slot, h, n):
        return jnp.dot(ks[slot][n:n + TILE], qs[h], preferred_element_type=jnp.float32)

    def absorb(slot, state, s, h, n):
        p = jnp.exp(s - refs[h])
        psum = jnp.sum(p.reshape(TILE // 8, 8, Q), axis=0)
        part = jnp.dot(
            vs[slot][h * HD:(h + 1) * HD, n:n + TILE], p.astype(jnp.bfloat16), preferred_element_type=jnp.float32)
        if n > 0:
            psum = psum + state[h][0]
            part = part + state[h][1]
        state[h] = (psum, part)
        if n + TILE == 1024:
            psums[h] = psum
            parts[h] = part

    def head(slot, h):
        psum, part = weigh(slot, h, refs[h], jnp.zeros((8, Q), jnp.float32), jnp.zeros((HD, Q), jnp.float32))
        psums[h] = psum
        parts[h] = part

    def restart(slot):
        for h in range(HEADS):
            s = jnp.dot(ks[slot][0:128], qs[h], preferred_element_type=jnp.float32)
            refs[h] = jnp.max(s, axis=0, keepdims=True)
            tot[h] = jnp.zeros((8, Q), jnp.float32)
            acc[h] = jnp.zeros((HD, Q), jnp.float32)

    def store(b):
        line = lax.broadcasted_iota(jnp.int32, (8, Q), 0)
        new = jnp.zeros((8, Q), jnp.float32)
        for h in range(HEADS):
            total = jnp.sum(tot[h], axis=0, keepdims=True)
            new = jnp.where(line == h, refs[h], jnp.where(line == 4 + h, total, new))
        st_out[b] = new
        w_out[b] = acc[...].reshape(DL, Q)

    def settle(slot, n):
        high = psums[0]
        for h in range(1, HEADS):
            high = jnp.maximum(high, psums[h])
        fine = jnp.max(high) < 1e20

        @pl.when(fine)
        def _():
            for h in range(HEADS):
                tot[h] += psums[h]
                acc[h] += parts[h]

        @pl.when(jnp.logical_not(fine))
        def _():
            for h in range(HEADS):
                top = refs[h]
                for n in range(0, 1024, TILE):
                    s = jnp.dot(ks[slot][n:n + TILE], qs[h], preferred_element_type=jnp.float32)
                    top = jnp.maximum(top, jnp.max(s, axis=0, keepdims=True))
                keep = jnp.exp(refs[h] - top)
                psum, part = weigh(slot, h, top, tot[h] * keep, acc[h] * keep)
                tot[h] = psum
                acc[h] = part
                refs[h] = top

        @pl.when(lax.rem(n, 3) == 2)
        def _():
            store(n // 3)

    def half(n, slot, begin):
        b = n // 3
        c = lax.rem(n, 3)
        other = 1 - slot

        @pl.when(c == 0)
        def _():
            outer_rows(b, lax.rem(b, 2))

        @pl.when(n >= 2)
        def _():
            out_copy(n - 2, slot).wait()

        @pl.when(jnp.logical_and(n > 0, lax.rem(n - 1, 3) == 0))
        def _():
            restart(other)

        if begin:
            @pl.when(n == 0)
            def _():
                for part in range(3):
                    inner_rows(0, 0, part)
                inner_rows(1, 1, 0)
                f0 = conv_of(b, c, 0)
                f1 = conv_of(b, c, 1)
                keep_features(f0, slot, 0)
                project(f0, slot, 0)
                keep_features(f1, slot, 1)
                project(f1, slot, 1)

        def mixed():
            after = jnp.minimum(b + 1, xt_ref.shape[0] - 1)
            next_slot = lax.rem(b + 1, 2)
            jobs = [(h, n) for h in range(HEADS) for n in range(0, 1024, TILE)]
            ahead = score(other, *jobs[0])
            state = {}
            now = ahead
            ahead = score(other, *jobs[1])
            f0 = conv_of(b, c, 0)
            absorb(other, state, now, *jobs[0])
            now = ahead
            ahead = score(other, *jobs[2])
            f1 = conv_of(b, c, 1)
            inner_rows(after, next_slot, c)
            absorb(other, state, now, *jobs[1])
            now = ahead
            ahead = score(other, *jobs[3])
            absorb(other, state, now, *jobs[2])
            now = ahead
            ahead = score(other, *jobs[4])
            keep_features(f0, slot, 0)
            project(f0, slot, 0)
            absorb(other, state, now, *jobs[3])
            now = ahead
            ahead = score(other, *jobs[5])
            absorb(other, state, now, *jobs[4])
            now = ahead
            ahead = score(other, *jobs[6])
            keep_features(f1, slot, 1)
            project(f1, slot, 1)
            absorb(other, state, now, *jobs[5])
            now = ahead
            ahead = score(other, *jobs[7])
            absorb(other, state, now, *jobs[6])
            now = ahead
            absorb(other, state, now, *jobs[7])

        if begin:
            pl.when(n > 0)(mixed)
        else:
            mixed()

        out_copy(n, slot).start()

        @pl.when(n > 0)
        def _():
            settle(other, n - 1)

    half(2 * step, 0, True)
    half(2 * step + 1, 1, False)

    @pl.when(step == NBLK // 2 - 1)
    def _():
        store(xt_ref.shape[0] - 1)
        k_out[...] = ks[1][...]
        v_out[...] = vs[1][...]
        q_out[...] = qs[...]
        out_copy(NBLK - 2, 0).wait()
        out_copy(NBLK - 1, 1).wait()


def encode(xt, rows, cols, w2, kt, vt, queries):
    samples = xt.shape[0]
    whole = pl.BlockSpec(memory_space=pltpu.VMEM)
    return pl.pallas_call(
        encode_kernel,
        grid=(NBLK // 2,),
        out_shape=(
            jax.ShapeDtypeStruct((samples, 128, 12, 2, 128), jnp.bfloat16),
            jax.ShapeDtypeStruct((samples, DL, Q), jnp.float32),
            jax.ShapeDtypeStruct((samples, 8, Q), jnp.float32),
            jax.ShapeDtypeStruct((1024, DL), jnp.bfloat16),
            jax.ShapeDtypeStruct((DL, 1024), jnp.bfloat16),
            jax.ShapeDtypeStruct((HEADS, DL, Q), jnp.bfloat16),
        ),
        in_specs=[whole] * 7,
        out_specs=(pl.BlockSpec(memory_space=pl.ANY),) + (whole,) * 5,
        scratch_shapes=[
            pltpu.VMEM((2, 26, KROW, 128), jnp.bfloat16),
            pltpu.VMEM((HEADS, DL, Q), jnp.bfloat16),
            pltpu.VMEM((1024, DL), jnp.bfloat16),
            pltpu.VMEM((1024, DL), jnp.bfloat16),
            pltpu.VMEM((DL, 1024), jnp.bfloat16),
            pltpu.VMEM((DL, 1024), jnp.bfloat16),
            pltpu.VMEM((128, 4, 2, 128), jnp.bfloat16),
            pltpu.VMEM((128, 4, 2, 128), jnp.bfloat16),
            pltpu.VMEM((HEADS, 1, Q), jnp.float32),
            pltpu.VMEM((HEADS, 8, Q), jnp.float32),
            pltpu.VMEM((HEADS, HD, Q), jnp.float32),
            pltpu.VMEM((HEADS, 8, Q), jnp.float32),
            pltpu.VMEM((HEADS, HD, Q), jnp.float32),
            pltpu.SemaphoreType.DMA((2,)),
        ],
        compiler_params=pltpu.CompilerParams(
            dimension_semantics=("arbitrary",), vmem_limit_bytes=40 * 1024 * 1024),
    )(xt, rows, cols, w2, kt, vt, queries)


def per_device(fields, conv_weight, kv_weight, out_weight, norm_gain, queries):
    samples, channels, lat_rows, lon_cols = fields.shape
    xt = jnp.pad(jnp.transpose(fields, (0, 2, 1, 3)), ((0, 0), (0, 0), (0, CP - channels), (0, 0)))
    conv_t = jnp.transpose(conv_weight, (0, 2, 1))
    rows, cols, w2, kt, vt = halo(xt, conv_t, kv_weight)
    feats, weighted, stats, keys, values, turned = encode(xt, rows, cols, w2, kt, vt, queries)
    features = feats.reshape(samples, 128, lat_rows, lon_cols)
    latents = reduce_all(weighted, stats, keys, values, turned, out_weight, norm_gain)
    return (features, latents)


def solution(mesh):
    in_specs = (P(None, None, "lat", "lon"), P(), P(), P(), P(), P())
    out_specs = (P(None, None, "lat", "lon"), P())
    return jax.shard_map(
        per_device, mesh=mesh, in_specs=in_specs, out_specs=out_specs, check_vma=False
    )
```

```python
import functools
import jax
import jax.numpy as jnp
from jax import lax
from jax.experimental import pallas as pl
from jax.experimental.pallas import tpu as pltpu
from jax.sharding import PartitionSpec as P

DL = 256
Q = 256
HEADS = 4
HD = 64
MESH = pl.DeviceIdType.MESH
ROWS = 8
NCHIP = 64


def reduce_kernel(
    w_in, st_in, k_ref, v_ref, q_ref, ow_ref, gain_ref, out_ref,
    w_ref, st_ref, half_w, half_st, msg, recv, gath,
    sem_a, sem_b, sem_c,
):
    lat = lax.axis_index("lat")
    lon = lax.axis_index("lon")
    core = lax.rem(lon, 2)
    chip = lat * 16 + lon // 2
    partner = lon + 1 - 2 * core

    def peer(k):
        c = lax.rem(chip + k, NCHIP)
        return (c // 16, lax.rem(c, 16) * 2 + core)

    barrier = pltpu.get_barrier_semaphore()
    pl.semaphore_signal(barrier, inc=1, device_id=(lat, partner), device_id_type=MESH)

    def greet(k, _):
        pl.semaphore_signal(barrier, inc=1, device_id=peer(k), device_id_type=MESH)
        return 0

    lax.fori_loop(1, NCHIP, greet, 0)

    def score(h):
        return jnp.dot(k_ref[...], q_ref[h], preferred_element_type=jnp.float32)

    tops, totals = [], []
    ahead = score(0)
    for h in range(HEADS):
        s = ahead
        if h + 1 < HEADS:
            ahead = score(h + 1)
        rows = slice(h * HD, (h + 1) * HD)
        before = st_in[3, h:h + 1]
        top = jnp.maximum(jnp.max(s, axis=0, keepdims=True), before)
        p = jnp.exp(s - top)
        shrink = jnp.exp(before - top)
        part = jnp.dot(v_ref[rows], p.astype(jnp.bfloat16), preferred_element_type=jnp.float32)
        w_ref[3, rows] = part + w_in[3, rows] * shrink
        tops.append(top)
        totals.append(jnp.sum(p, axis=0, keepdims=True) + st_in[3, 4 + h:5 + h] * shrink)
    st_ref[3] = jnp.concatenate(tops + totals, axis=0)
    for i in range(3):
        w_ref[i] = w_in[i]
        st_ref[i] = st_in[i]
    pl.semaphore_wait(barrier, NCHIP)

    give = 2 - 2 * core
    keep = 2 * core
    cs = pltpu.make_async_remote_copy(
        st_ref.at[pl.ds(give, 2)], half_st, sem_a.at[0], sem_a.at[1],
        device_id=(lat, partner), device_id_type=MESH)
    cw = [
        pltpu.make_async_remote_copy(
            w_ref.at[give + i], half_w.at[i], sem_a.at[2 + 2 * i], sem_a.at[3 + 2 * i],
            device_id=(lat, partner), device_id_type=MESH)
        for i in range(2)
    ]
    cs.start()
    for c in cw:
        c.start()

    def limbs(v):
        a = v.astype(jnp.bfloat16).astype(jnp.float32)
        b = (v - a).astype(jnp.bfloat16).astype(jnp.float32)
        return [a, b, v - a - b]

    cs.wait()
    for i in range(2):
        s1 = st_ref[keep + i]
        s2 = half_st[i]
        peak = jnp.maximum(s1[0:4], s2[0:4])
        f1 = jnp.exp(s1[0:4] - peak)
        f2 = jnp.exp(s2[0:4] - peak)
        total = s1[4:8] * f1 + s2[4:8] * f2
        cw[i].wait()
        for h in range(HEADS):
            line = slice(h, h + 1)
            rows = slice(h * HD, (h + 1) * HD)
            value = w_ref[keep + i, rows] * f1[line] + half_w[i, rows] * f2[line]
            first = i * 32 + h * 8
            msg[first:first + 8, 0:ROWS] = value.reshape(8, ROWS, Q).astype(jnp.bfloat16)
            extra = jnp.concatenate(
                limbs(peak[line]) + limbs(total[line]) + [jnp.zeros((2, Q), jnp.float32)], axis=0)
            msg[first:first + 8, ROWS:2 * ROWS] = jnp.broadcast_to(extra[None], (8, ROWS, Q)).astype(jnp.bfloat16)

    def scatter(k, _):
        c = lax.rem(chip + k, NCHIP)
        pltpu.make_async_remote_copy(
            msg.at[c], recv.at[k - 1], sem_b.at[0], sem_b.at[1], device_id=peer(k), device_id_type=MESH).start()
        return 0

    lax.fori_loop(1, NCHIP, scatter, 0)
    own = msg[chip].astype(jnp.float32)
    pltpu.make_async_copy(recv, recv, sem_b.at[1]).wait()

    got = recv[...].astype(jnp.float32)
    extra = got[:, ROWS:2 * ROWS]
    m = extra[:, 0:1] + extra[:, 1:2] + extra[:, 2:3]
    t = extra[:, 3:4] + extra[:, 4:5] + extra[:, 5:6]
    own_m = own[8:9] + own[9:10] + own[10:11]
    own_t = own[11:12] + own[12:13] + own[13:14]
    top = jnp.maximum(jnp.max(m, axis=0), own_m)
    fac = jnp.exp(m - top[None])
    own_fac = jnp.exp(own_m - top)
    total = jnp.sum(fac * t, axis=0) + own_fac * own_t
    summed = jnp.sum(got[:, 0:ROWS] * fac, axis=0) + own[0:ROWS] * own_fac
    mine = core * NCHIP + chip
    gath[mine] = (summed / total).astype(jnp.bfloat16)

    def spread(k, _):
        pltpu.make_async_remote_copy(
            gath.at[mine], gath.at[mine], sem_c.at[0], sem_c.at[1], device_id=peer(k), device_id_type=MESH).start()
        return 0

    lax.fori_loop(1, NCHIP, spread, 0)
    pltpu.make_async_copy(recv, recv, sem_b.at[0]).wait()
    size = gath.at[pl.ds(0, NCHIP - 1)]
    pltpu.make_async_copy(size, size, sem_c.at[1]).wait()
    block = gath.at[pl.ds(core * NCHIP, NCHIP)]
    cg = pltpu.make_async_remote_copy(
        block, block, sem_c.at[2], sem_c.at[3], device_id=(lat, partner), device_id_type=MESH)
    cg.start()

    def finish(b):
        att = gath[pl.ds(b * 32, 32)].astype(jnp.float32).reshape(DL, Q).T.astype(jnp.bfloat16)
        proj = jnp.dot(att, ow_ref[...], preferred_element_type=jnp.float32)
        out_ref[b] = (
            proj * lax.rsqrt(jnp.mean(proj * proj, axis=-1, keepdims=True) + 1e-06) * gain_ref[...]
        )

    finish(keep)
    finish(keep + 1)
    cg.wait()
    finish(give)
    finish(give + 1)
    pltpu.make_async_copy(size, size, sem_c.at[0]).wait()


def reduce_all(weighted, stats, keys, values, turned, out_weight, norm_gain):
    vm = pl.BlockSpec(memory_space=pltpu.VMEM)
    return pl.pallas_call(
        reduce_kernel,
        out_shape=jax.ShapeDtypeStruct((4, Q, DL), jnp.float32),
        in_specs=[vm] * 7,
        out_specs=vm,
        scratch_shapes=[
            pltpu.VMEM((4, DL, Q), jnp.float32),
            pltpu.VMEM((4, 8, Q), jnp.float32),
            pltpu.VMEM((2, DL, Q), jnp.float32),
            pltpu.VMEM((2, 8, Q), jnp.float32),
            pltpu.VMEM((NCHIP, 2 * ROWS, Q), jnp.bfloat16),
            pltpu.VMEM((NCHIP - 1, 2 * ROWS, Q), jnp.bfloat16),
            pltpu.VMEM((2 * NCHIP, ROWS, Q), jnp.bfloat16),
            pltpu.SemaphoreType.DMA((6,)),
            pltpu.SemaphoreType.DMA((2,)),
            pltpu.SemaphoreType.DMA((4,)),
        ],
        compiler_params=pltpu.CompilerParams(
            collective_id=1, has_side_effects=True, vmem_limit_bytes=32 * 1024 * 1024
        ),
    )(weighted, stats, keys, values, turned, out_weight, norm_gain.reshape(1, DL))


CP = 80
KROW = 3 * CP
SCALE = HD ** (-0.5)
NT = (((1,), (1,)), ((), ()))


def halo_kernel(
    xt_ref, cw_ref, kv_ref, rows_ref, cols_ref, w2_ref, kt_ref, vt_ref,
    edge, got, taps, send_sem, recv_sem,
):
    lat = lax.axis_index("lat")
    lon = lax.axis_index("lon")
    nlat = lax.axis_size("lat")
    nlon = lax.axis_size("lon")
    right = lax.rem(lon + 1, nlon)
    left = lax.rem(lon + nlon - 1, nlon)
    barrier = pltpu.get_barrier_semaphore()

    def greet(dlat, dlon):
        pl.semaphore_signal(barrier, inc=1, device_id=(dlat, dlon), device_id_type=MESH)

    greet(lat, left)
    greet(lat, right)

    @pl.when(lat > 0)
    def _():
        greet(lat - 1, left)
        greet(lat - 1, lon)
        greet(lat - 1, right)

    @pl.when(lat < nlat - 1)
    def _():
        greet(lat + 1, left)
        greet(lat + 1, lon)
        greet(lat + 1, right)

    lane = lax.broadcasted_iota(jnp.int32, (CP, 128), 1)
    last = jnp.zeros((CP, 128), jnp.float32)
    first = jnp.zeros((CP, 128), jnp.float32)
    for b in range(xt_ref.shape[0]):
        for i in range(24):
            at = b * 24 + i
            row = xt_ref[b, i].astype(jnp.float32)
            turned = pltpu.roll(row, at + 1, 1)
            last = jnp.where(lane == at, turned, last)
            first = jnp.where(lane == at + 1, turned, first)
    edge[0] = last.astype(jnp.bfloat16)
    edge[1] = first.astype(jnp.bfloat16)

    def copy(src, dst, n, dlat, dlon):
        return pltpu.make_async_remote_copy(
            src, dst, send_sem.at[n], recv_sem.at[n], device_id=(dlat, dlon), device_id_type=MESH)

    same = [
        copy(edge.at[0], got.at[0, 0], 0, lat, right),
        copy(edge.at[1], got.at[1, 0], 1, lat, left),
    ]
    down = [
        copy(xt_ref.at[:, 23], rows_ref.at[0], 2, lat + 1, lon),
        copy(edge.at[0], got.at[0, 1], 3, lat + 1, right),
        copy(edge.at[1], got.at[1, 1], 4, lat + 1, left),
    ]
    up = [
        copy(xt_ref.at[:, 0], rows_ref.at[1], 5, lat - 1, lon),
        copy(edge.at[0], got.at[0, 2], 6, lat - 1, right),
        copy(edge.at[1], got.at[1, 2], 7, lat - 1, left),
    ]
    inner = jnp.logical_and(lat > 0, lat < nlat - 1)

    @pl.when(inner)
    def _():
        pl.semaphore_wait(barrier, 8)

    @pl.when(jnp.logical_not(inner))
    def _():
        pl.semaphore_wait(barrier, 5)

    for c in same:
        c.start()

    @pl.when(lat < nlat - 1)
    def _():
        for c in down:
            c.start()

    @pl.when(lat > 0)
    def _():
        for c in up:
            c.start()

    taps[...] = jnp.zeros_like(taps)
    for t in range(9):
        value = cw_ref[t].astype(jnp.float32)
        value = jnp.concatenate([value, jnp.zeros((CP - value.shape[0], 128), jnp.float32)], axis=0).astype(jnp.bfloat16)
        taps[t * CP:(t + 1) * CP, 0:128] = value
        taps[KROW + t * CP:KROW + (t + 1) * CP, 128:256] = value
    out_at = lax.broadcasted_iota(jnp.int32, (256, 256), 0)
    in_at = lax.broadcasted_iota(jnp.int32, (256, 256), 1)
    spread = jnp.where(out_at == jnp.where(in_at < 128, 2 * in_at, 2 * in_at - 255), 1.0, 0.0).astype(jnp.bfloat16)
    w2_ref[...] = lax.dot_general(spread, taps[...], NT, preferred_element_type=jnp.float32).astype(jnp.bfloat16)
    for r in range(2):
        some = spread[:, r * 128:(r + 1) * 128]
        kt_ref[:, r * DL:(r + 1) * DL] = lax.dot_general(
            some, kv_ref[0:DL], NT, preferred_element_type=jnp.float32).astype(jnp.bfloat16)
        vt_ref[r * DL:(r + 1) * DL] = lax.dot_general(
            kv_ref[DL:2 * DL], some, NT, preferred_element_type=jnp.float32).astype(jnp.bfloat16)

    for c in same:
        c.wait()

    @pl.when(lat > 0)
    def _():
        for c in down:
            c.wait_recv()
        for c in up:
            c.wait_send()

    @pl.when(lat < nlat - 1)
    def _():
        for c in up:
            c.wait_recv()
        for c in down:
            c.wait_send()

    @pl.when(lat == 0)
    def _():
        rows_ref[0] = jnp.zeros_like(rows_ref[0])
        for side in range(2):
            got[side, 1] = jnp.zeros((CP, 128), jnp.bfloat16)

    @pl.when(lat == nlat - 1)
    def _():
        rows_ref[1] = jnp.zeros_like(rows_ref[1])
        for side in range(2):
            got[side, 2] = jnp.zeros((CP, 128), jnp.bfloat16)

    for side in range(2):
        mid = got[side, 0].astype(jnp.float32)
        above = got[side, 1].astype(jnp.float32)
        below = got[side, 2].astype(jnp.float32)
        for b in range(4):
            at = b * 24 + side
            value = pltpu.roll(mid, (129 - at) % 128, 1)
            value = jnp.where(lane == 0, pltpu.roll(above, (128 - at - 23) % 128, 1), value)
            value = jnp.where(lane == 25, pltpu.roll(below, (128 + 25 - at) % 128, 1), value)
            cols_ref[side, b] = value.astype(jnp.bfloat16)


def halo(xt, conv_t, kv_weight):
    vm = pl.BlockSpec(memory_space=pltpu.VMEM)
    samples = xt.shape[0]
    return pl.pallas_call(
        halo_kernel,
        out_shape=(
            jax.ShapeDtypeStruct((2, samples, CP, 128), jnp.bfloat16),
            jax.ShapeDtypeStruct((2, samples, CP, 128), jnp.bfloat16),
            jax.ShapeDtypeStruct((256, 4 * KROW), jnp.bfloat16),
            jax.ShapeDtypeStruct((256, 512), jnp.bfloat16),
            jax.ShapeDtypeStruct((512, 256), jnp.bfloat16),
        ),
        in_specs=[vm] * 3,
        out_specs=(vm,) * 5,
        scratch_shapes=[
            pltpu.VMEM((2, CP, 128), jnp.bfloat16),
            pltpu.VMEM((2, 3, CP, 128), jnp.bfloat16),
            pltpu.VMEM((4 * KROW, 256), jnp.bfloat16),
            pltpu.SemaphoreType.DMA((8,)),
            pltpu.SemaphoreType.DMA((8,)),
        ],
        compiler_params=pltpu.CompilerParams(
            collective_id=0, has_side_effects=True, vmem_limit_bytes=32 * 1024 * 1024),
    )(xt, conv_t, kv_weight)


NBLK = 12
TILE = 512


def encode_kernel(
    xt_ref, rows_ref, cols_ref, w2_ref, kt_ref, vt_ref, q_ref, feat_ref, w_out, st_out, k_out, v_out, q_out,
    x3, qs, k_a, k_b, v_a, v_b, feat_a, feat_b, refs, tot, acc, psums, parts, sem,
):
    step = pl.program_id(0)
    ks = (k_a, k_b)
    vs = (v_a, v_b)
    fbuf = (feat_a, feat_b)
    lane = lax.broadcasted_iota(jnp.int32, (CP, 128), 1)

    @pl.when(step == 0)
    def _():
        turned = (q_ref[...].astype(jnp.float32) * SCALE).T
        owner = lax.broadcasted_iota(jnp.int32, (DL, Q), 0) // HD
        for h in range(HEADS):
            qs[h] = jnp.where(owner == h, turned, 0.0).astype(jnp.bfloat16)

    def put_row(slot, i, row, lo, hi):
        before = jnp.where(lane == 0, lo, pltpu.roll(row, 1, 1))
        after = jnp.where(lane == 127, hi, pltpu.roll(row, 127, 1))
        x3[slot, i, 0:CP] = before
        x3[slot, i, CP:2 * CP] = row
        x3[slot, i, 2 * CP:3 * CP] = after

    def outer_rows(b, slot):
        lo = cols_ref[0, b]
        hi = cols_ref[1, b]
        put_row(slot, 0, rows_ref[0, b], lo, pltpu.roll(hi, 127, 1))
        put_row(slot, 25, rows_ref[1, b], pltpu.roll(lo, 103, 1), pltpu.roll(hi, 102, 1))

    def inner_rows(b, slot, c):
        lo = pltpu.roll(cols_ref[0, b], 128 - 8 * c, 1) if isinstance(c, int) and c > 0 else cols_ref[0, b]
        hi = pltpu.roll(cols_ref[1, b], 128 - 8 * c, 1) if isinstance(c, int) and c > 0 else cols_ref[1, b]
        if not isinstance(c, int):
            lo = pltpu.roll(lo.astype(jnp.float32), lax.rem(128 - 8 * c, 128), 1).astype(jnp.bfloat16)
            hi = pltpu.roll(hi.astype(jnp.float32), lax.rem(128 - 8 * c, 128), 1).astype(jnp.bfloat16)
        for j in range(8):
            put_row(slot, 8 * c + 1 + j, xt_ref[b, 8 * c + j],
                    pltpu.roll(lo, 127 - j, 1), pltpu.roll(hi, 126 - j, 1))

    def out_copy(n, slot):
        return pltpu.make_async_copy(
            fbuf[slot], feat_ref.at[n // 3, :, pl.ds(lax.rem(n, 3) * 4, 4)], sem.at[slot])

    def conv_of(b, c, g):
        base = c * 8 + g * 4
        one = x3[lax.rem(b, 2), pl.ds(base, 4)].reshape(4 * KROW, 128)
        two = x3[lax.rem(b, 2), pl.ds(base + 2, 4)].reshape(4 * KROW, 128)
        both = jnp.concatenate([one, two], axis=1)
        conv = jnp.dot(w2_ref[...], both, preferred_element_type=jnp.float32)
        return jax.nn.gelu(conv, approximate=True).astype(jnp.bfloat16)

    def keep_features(feats, slot, g):
        fbuf[slot][:, 2 * g] = feats[:, 0:128].reshape(128, 2, 128)
        fbuf[slot][:, 2 * g + 1] = feats[:, 128:256].reshape(128, 2, 128)

    def project(feats, slot, g):
        turned = feats.T
        values = jnp.dot(vt_ref[...], feats, preferred_element_type=jnp.float32).astype(jnp.bfloat16)
        keys = jnp.dot(turned, kt_ref[...], preferred_element_type=jnp.float32).astype(jnp.bfloat16)
        for r in range(2):
            at = r * 512 + g * 256
            vs[slot][:, at:at + 256] = values[r * DL:(r + 1) * DL]
            ks[slot][at:at + 256] = keys[:, r * DL:(r + 1) * DL]

    def weigh(slot, h, ref, psum, part):
        for n in range(0, 1024, TILE):
            s = jnp.dot(ks[slot][n:n + TILE], qs[h], preferred_element_type=jnp.float32)
            p = jnp.exp(s - ref)
            psum = psum + jnp.sum(p.reshape(TILE // 8, 8, Q), axis=0)
            part = part + jnp.dot(
                vs[slot][h * HD:(h + 1) * HD, n:n + TILE], p.astype(jnp.bfloat16), preferred_element_type=jnp.float32)
        return psum, part

    def score(slot, h, n):
        return jnp.dot(ks[slot][n:n + TILE], qs[h], preferred_element_type=jnp.float32)

    def absorb(slot, state, s, h, n):
        p = jnp.exp(s - refs[h])
        psum = jnp.sum(p.reshape(TILE // 8, 8, Q), axis=0)
        part = jnp.dot(
            vs[slot][h * HD:(h + 1) * HD, n:n + TILE], p.astype(jnp.bfloat16), preferred_element_type=jnp.float32)
        if n > 0:
            psum = psum + state[h][0]
            part = part + state[h][1]
        state[h] = (psum, part)
        if n + TILE == 1024:
            psums[h] = psum
            parts[h] = part

    def head(slot, h):
        psum, part = weigh(slot, h, refs[h], jnp.zeros((8, Q), jnp.float32), jnp.zeros((HD, Q), jnp.float32))
        psums[h] = psum
        parts[h] = part

    def restart(slot):
        for h in range(HEADS):
            s = jnp.dot(ks[slot][0:128], qs[h], preferred_element_type=jnp.float32)
            refs[h] = jnp.max(s, axis=0, keepdims=True)
            tot[h] = jnp.zeros((8, Q), jnp.float32)
            acc[h] = jnp.zeros((HD, Q), jnp.float32)

    def store(b):
        line = lax.broadcasted_iota(jnp.int32, (8, Q), 0)
        new = jnp.zeros((8, Q), jnp.float32)
        for h in range(HEADS):
            total = jnp.sum(tot[h], axis=0, keepdims=True)
            new = jnp.where(line == h, refs[h], jnp.where(line == 4 + h, total, new))
        st_out[b] = new
        w_out[b] = acc[...].reshape(DL, Q)

    def settle(slot, n):
        high = psums[0]
        for h in range(1, HEADS):
            high = jnp.maximum(high, psums[h])
        fine = jnp.max(high) < 1e20

        @pl.when(fine)
        def _():
            for h in range(HEADS):
                tot[h] += psums[h]
                acc[h] += parts[h]

        @pl.when(jnp.logical_not(fine))
        def _():
            for h in range(HEADS):
                top = refs[h]
                for n in range(0, 1024, TILE):
                    s = jnp.dot(ks[slot][n:n + TILE], qs[h], preferred_element_type=jnp.float32)
                    top = jnp.maximum(top, jnp.max(s, axis=0, keepdims=True))
                keep = jnp.exp(refs[h] - top)
                psum, part = weigh(slot, h, top, tot[h] * keep, acc[h] * keep)
                tot[h] = psum
                acc[h] = part
                refs[h] = top

        @pl.when(lax.rem(n, 3) == 2)
        def _():
            store(n // 3)

    def half(n, slot, begin):
        b = n // 3
        c = lax.rem(n, 3)
        other = 1 - slot

        @pl.when(c == 0)
        def _():
            outer_rows(b, lax.rem(b, 2))

        @pl.when(n >= 2)
        def _():
            out_copy(n - 2, slot).wait()

        @pl.when(jnp.logical_and(n > 0, lax.rem(n - 1, 3) == 0))
        def _():
            restart(other)

        if begin:
            @pl.when(n == 0)
            def _():
                inner_rows(0, 0, 0)
                inner_rows(0, 0, 1)
                f0 = conv_of(b, c, 0)
                f1 = conv_of(b, c, 1)
                inner_rows(0, 0, 2)
                inner_rows(1, 1, 0)
                keep_features(f0, slot, 0)
                project(f0, slot, 0)
                keep_features(f1, slot, 1)
                project(f1, slot, 1)

        def mixed():
            after = jnp.minimum(b + 1, xt_ref.shape[0] - 1)
            next_slot = lax.rem(b + 1, 2)
            jobs = [(h, n) for h in range(HEADS) for n in range(0, 1024, TILE)]
            ahead = score(other, *jobs[0])
            state = {}
            now = ahead
            ahead = score(other, *jobs[1])
            f0 = conv_of(b, c, 0)
            absorb(other, state, now, *jobs[0])
            now = ahead
            ahead = score(other, *jobs[2])
            f1 = conv_of(b, c, 1)
            inner_rows(after, next_slot, c)
            absorb(other, state, now, *jobs[1])
            now = ahead
            ahead = score(other, *jobs[3])
            absorb(other, state, now, *jobs[2])
            now = ahead
            ahead = score(other, *jobs[4])
            keep_features(f0, slot, 0)
            project(f0, slot, 0)
            absorb(other, state, now, *jobs[3])
            now = ahead
            ahead = score(other, *jobs[5])
            absorb(other, state, now, *jobs[4])
            now = ahead
            ahead = score(other, *jobs[6])
            keep_features(f1, slot, 1)
            project(f1, slot, 1)
            absorb(other, state, now, *jobs[5])
            now = ahead
            ahead = score(other, *jobs[7])
            absorb(other, state, now, *jobs[6])
            now = ahead
            absorb(other, state, now, *jobs[7])

        if begin:
            pl.when(n > 0)(mixed)
        else:
            mixed()

        out_copy(n, slot).start()

        @pl.when(n > 0)
        def _():
            settle(other, n - 1)

    half(2 * step, 0, True)
    half(2 * step + 1, 1, False)

    @pl.when(step == NBLK // 2 - 1)
    def _():
        store(xt_ref.shape[0] - 1)
        k_out[...] = ks[1][...]
        v_out[...] = vs[1][...]
        q_out[...] = qs[...]
        out_copy(NBLK - 2, 0).wait()
        out_copy(NBLK - 1, 1).wait()


def encode(xt, rows, cols, w2, kt, vt, queries):
    samples = xt.shape[0]
    whole = pl.BlockSpec(memory_space=pltpu.VMEM)
    return pl.pallas_call(
        encode_kernel,
        grid=(NBLK // 2,),
        out_shape=(
            jax.ShapeDtypeStruct((samples, 128, 12, 2, 128), jnp.bfloat16),
            jax.ShapeDtypeStruct((samples, DL, Q), jnp.float32),
            jax.ShapeDtypeStruct((samples, 8, Q), jnp.float32),
            jax.ShapeDtypeStruct((1024, DL), jnp.bfloat16),
            jax.ShapeDtypeStruct((DL, 1024), jnp.bfloat16),
            jax.ShapeDtypeStruct((HEADS, DL, Q), jnp.bfloat16),
        ),
        in_specs=[whole] * 7,
        out_specs=(pl.BlockSpec(memory_space=pl.ANY),) + (whole,) * 5,
        scratch_shapes=[
            pltpu.VMEM((2, 26, KROW, 128), jnp.bfloat16),
            pltpu.VMEM((HEADS, DL, Q), jnp.bfloat16),
            pltpu.VMEM((1024, DL), jnp.bfloat16),
            pltpu.VMEM((1024, DL), jnp.bfloat16),
            pltpu.VMEM((DL, 1024), jnp.bfloat16),
            pltpu.VMEM((DL, 1024), jnp.bfloat16),
            pltpu.VMEM((128, 4, 2, 128), jnp.bfloat16),
            pltpu.VMEM((128, 4, 2, 128), jnp.bfloat16),
            pltpu.VMEM((HEADS, 1, Q), jnp.float32),
            pltpu.VMEM((HEADS, 8, Q), jnp.float32),
            pltpu.VMEM((HEADS, HD, Q), jnp.float32),
            pltpu.VMEM((HEADS, 8, Q), jnp.float32),
            pltpu.VMEM((HEADS, HD, Q), jnp.float32),
            pltpu.SemaphoreType.DMA((2,)),
        ],
        compiler_params=pltpu.CompilerParams(
            dimension_semantics=("arbitrary",), vmem_limit_bytes=40 * 1024 * 1024),
    )(xt, rows, cols, w2, kt, vt, queries)


def per_device(fields, conv_weight, kv_weight, out_weight, norm_gain, queries):
    samples, channels, lat_rows, lon_cols = fields.shape
    xt = jnp.pad(jnp.transpose(fields, (0, 2, 1, 3)), ((0, 0), (0, 0), (0, CP - channels), (0, 0)))
    conv_t = jnp.transpose(conv_weight, (0, 2, 1))
    rows, cols, w2, kt, vt = halo(xt, conv_t, kv_weight)
    feats, weighted, stats, keys, values, turned = encode(xt, rows, cols, w2, kt, vt, queries)
    features = feats.reshape(samples, 128, lat_rows, lon_cols)
    latents = reduce_all(weighted, stats, keys, values, turned, out_weight, norm_gain)
    return (features, latents)


def solution(mesh):
    in_specs = (P(None, None, "lat", "lon"), P(), P(), P(), P(), P())
    out_specs = (P(None, None, "lat", "lon"), P())
    return jax.shard_map(
        per_device, mesh=mesh, in_specs=in_specs, out_specs=out_specs, check_vma=False
    )
```
